32 devices in a mesh: groups: 2 (over y), dom: 4 (over z), sub: 2 (over x), chip: 2 (over core).
Axes of the slice: x: 2, y: 2, z: 4, core: 2. Of those that a mesh axis runs over, the one named last changes fastest.
Arguments:
- field_prev: float32 [16, 16384], P(('groups', 'dom', 'sub')), parts along dimension 0, may hold values from -6 to 6
- field_now: float32 [16, 16384], P(('groups', 'dom', 'sub')), parts along dimension 0, may hold values from -6 to 6
- adjoint_now: float32 [16, 16384], P(('groups', 'dom', 'sub')), parts along dimension 0, may hold values from -6 to 6
- adjoint_next: float32 [16, 16384], P(('groups', 'dom', 'sub')), parts along dimension 0, may hold values from -6 to 6
- inv_mass: float32 [16, 16384], P(('groups', 'dom', 'sub')), parts along dimension 0, may hold values from 0.02 to 0.2
- metric: float32 [2048, 1536], P(('groups', 'dom', 'sub', 'chip')), parts along dimension 0, may hold values from 0.25 to 4
- connect: int32 [2048, 512], P(('groups', 'dom', 'sub', 'chip')), parts along dimension 0, may hold values from 0 to 16383
- surface: float32 [2048, 512], P(('groups', 'dom', 'sub', 'chip')), parts along dimension 0, may hold values from 0.5 to 4
- driver: int32 [2048], P(('groups', 'dom', 'sub', 'chip')), parts along dimension 0, may hold values from 0 to 31
- shared: int32 [16, 3, 2, 512], P(('groups', 'dom', 'sub')), parts along dimension 0, may hold values from 0 to 16384, as said below
- filter_taps: float32 [8, 2048], P(None, ('dom', 'sub', 'chip')), may hold values from -0.125 to 0.125
- signal: float32 [2, 2048], replicated, may hold values from -6 to 6
Outputs:
- field_out: float32 [16, 16384], P(('groups', 'dom', 'sub')), parts along dimension 0
- adjoint_out: float32 [16, 16384], P(('groups', 'dom', 'sub')), parts along dimension 0
- filter_grad: float32 [16, 2048], P('groups', ('dom', 'sub', 'chip')), parts along dimension 0
The draws below stay inside these ranges and needn't reach their ends.
There are 2 independent parts, one for each index of `groups`. The reference program is written for one: setup_inputs(seed, part) draws one part's arguments, and reference() takes and returns one part's arrays. A program takes and returns all parts, laid end to end along the dimension named above; an argument that names none is the same for every part. Nothing has to cross between parts.
Inputs may be any that keep to these rules, and one draw needn't show every extreme that they name: `connect`: local node numbers of the element's own partition. A value below 8 names the driver on whose surface the element lies; 8 or more means none. shared[p, o, j, :] lists the nodes that partition p shares with partition (d + o - 1) * 2 + j, live entries first, then the value 16384 in every empty slot. The list of p toward q and the list of q toward p hold the same number of live entries and pair position by position. Slots toward a dom index outside the grid and toward p itself are empty. A list holds at most 512 live entries, and in every dom layer some pair holds exactly 512.
All inputs are finite; a program needn't handle non-finite values.
Results may differ from the reference program's by a relative error of at most 0.0001.
Values sent between devices are 32-bit elements; how exact they have to be, the bound alone decides.
No kernel may reach another device: no remote copies, remote signals or barrier semaphores. Data moves between devices by JAX's collectives and lax.ppermute only.
A program may use at most 128 MiB of HBM per device.

```python
import math
import jax
import jax.numpy as jnp
import numpy as np
from jax import lax

ELEM_NODES = 512
CAP = 512
STEPS = 2
DRIVERS = 8
TAPS = 2048
PART_NODES = 16384
NPART = 8
ELEMS = 1024
N_DOM = 4
N_SUB = 2


def draw_shared(key, part):
    key = jax.random.fold_in(key, 7)
    keys = jax.random.split(key, 7)
    shape = (N_DOM, N_SUB, N_SUB)
    same = jax.random.randint(keys[0], shape, CAP // 4, CAP + 1)
    same = jnp.where(jax.random.randint(keys[1], shape, 0, 4) > 0, same, 0)
    row_ids = jnp.arange(N_SUB)[None, :, None]
    column_ids = jnp.arange(N_SUB)[None, None, :]
    same = jnp.where(row_ids < column_ids, same, jnp.swapaxes(same, 1, 2))
    same = jnp.where(row_ids == column_ids, 0, same)
    first = jax.random.randint(keys[2], (N_DOM, 1, 1), 0, N_SUB)
    second = (first + jax.random.randint(keys[3], (N_DOM, 1, 1), 1, N_SUB)) % N_SUB
    full_pair = (row_ids == first) & (column_ids == second) | (row_ids == second) & (column_ids == first)
    same = jnp.where(full_pair, CAP, same)
    upward = jax.random.randint(keys[4], shape, CAP // 4, CAP + 1)
    upward = jnp.where(jax.random.randint(keys[5], shape, 0, 4) > 0, upward, 0)
    blank = jnp.zeros((1, N_SUB, N_SUB), jnp.int32)
    below = jnp.concatenate([blank, jnp.swapaxes(upward[:-1], 1, 2)], axis=0)
    above = jnp.concatenate([upward[:-1], blank], axis=0)
    counts = jnp.stack([below, same, above], axis=2)
    picks = jax.random.randint(keys[6], (N_DOM, N_SUB, 3, N_SUB, CAP), 0, PART_NODES)
    slots = jnp.arange(CAP)
    result = jnp.where(slots < counts[..., None], picks, PART_NODES)
    return result.reshape(N_DOM * N_SUB, 3, N_SUB, CAP).astype(jnp.int32)


def set_ends(entries, key, low, largest):
    longest = entries.shape.index(max(entries.shape))
    spots = []
    for shift in (0, 1):
        where = [jax.random.randint(jax.random.fold_in(key, axis), (), 0, length) for axis, length in enumerate(entries.shape)]
        where[longest] = (where[longest] + shift) % entries.shape[longest]
        spots.append(tuple(where))
    return entries.at[spots[0]].set(low).at[spots[1]].set(largest)


def level_of(key, shape, pieces, least, top_value):
    loudness = 1.0
    for dim, blocks in pieces:
        steps = jax.random.uniform(jax.random.fold_in(jax.random.fold_in(key, 6), dim), (blocks,), jnp.float32, least / len(pieces), top_value / len(pieces))
        loudness = loudness * jnp.repeat(jnp.exp(steps), shape[dim] // blocks).reshape((-1,) + (1,) * (len(shape) - 1 - dim))
    return loudness


def bell_draw(rng, shape, spread, limit, cuts=(), held_as=jnp.bfloat16):
    gain = level_of(rng, shape, cuts, -0.22, 0.18) if cuts else 1.0
    entries = jax.random.normal(rng, shape, jnp.float32) * spread * gain
    return jnp.minimum(jnp.maximum(entries, -limit), limit).astype(held_as)


def setup_inputs(seed: int = 0, part: int = 0) -> dict:
    arg_keys = jax.random.split(jax.random.key(seed), 13)
    own_keys = jax.random.split(jax.random.fold_in(arg_keys[12], part), 13)
    field_prev = bell_draw(own_keys[0], (NPART, PART_NODES), 1.0, 6.0, ((0, 8),), jnp.float32)
    field_now = bell_draw(own_keys[1], (NPART, PART_NODES), 1.0, 6.0, ((0, 8),), jnp.float32)
    adjoint_now = bell_draw(own_keys[2], (NPART, PART_NODES), 1.0, 6.0, ((0, 8),), jnp.float32)
    adjoint_next = bell_draw(own_keys[3], (NPART, PART_NODES), 1.0, 6.0, ((0, 8),), jnp.float32)
    inv_mass = jnp.clip(jnp.exp(math.log(0.2) - 2.3025851 * jax.random.uniform(own_keys[4], (NPART, PART_NODES), jnp.float32) ** level_of(own_keys[4], (NPART, PART_NODES), ((0, 8),), -0.2, 0.2)), 0.02, 0.2)
    metric = jnp.clip(jnp.exp(math.log(4.0) - 2.7725887 * jax.random.uniform(own_keys[5], (ELEMS, 3 * ELEM_NODES), jnp.float32) ** level_of(own_keys[5], (ELEMS, 3 * ELEM_NODES), ((0, 16),), -0.2, 0.2)), 0.25, 4.0)
    connect = set_ends(jax.random.randint(own_keys[6], (ELEMS, ELEM_NODES), 0, PART_NODES), jax.random.fold_in(own_keys[6], 1), 0, PART_NODES - 1).astype(jnp.int32)
    surface = jnp.clip(jnp.exp(math.log(4.0) - 2.0794415 * jax.random.uniform(own_keys[7], (ELEMS, ELEM_NODES), jnp.float32) ** level_of(own_keys[7], (ELEMS, ELEM_NODES), ((0, 16),), -0.2, 0.2)), 0.5, 4.0)
    driver = set_ends(jax.random.randint(own_keys[8], (ELEMS,), 0, 4 * DRIVERS), jax.random.fold_in(own_keys[8], 1), 0, (4 * DRIVERS) - 1).astype(jnp.int32)
    shared = draw_shared(jax.random.fold_in(jax.random.fold_in(arg_keys[12], part), 71), part)
    filter_taps = bell_draw(arg_keys[10], (DRIVERS, TAPS), TAPS ** -0.5, 0.125, ((1, 16),), jnp.float32)
    signal = bell_draw(arg_keys[11], (STEPS, TAPS), 1.0, 6.0, (), jnp.float32)
    return dict(field_prev=field_prev, field_now=field_now, adjoint_now=adjoint_now, adjoint_next=adjoint_next, inv_mass=inv_mass, metric=metric, connect=connect, surface=surface, driver=driver, shared=shared, filter_taps=filter_taps, signal=signal)


GLL_POINTS = (-1.0, -0.8717401485096066, -0.5917001814331423, -0.2092992179024789, 0.2092992179024789, 0.5917001814331423, 0.8717401485096066, 1.0)
GLL_WEIGHTS = (0.03571428571428571, 0.21070422714350603, 0.3411226924835044, 0.4124587946587038, 0.4124587946587038, 0.3411226924835044, 0.21070422714350603, 0.03571428571428571)

def element_tables():
    points = np.array(GLL_POINTS)
    identity = np.eye(8)
    diffs = points[:, None] - points[None, :] + identity
    barycentric = 1.0 / np.prod(diffs, axis=1)
    derivative = barycentric[None, :] / barycentric[:, None] / diffs
    derivative = derivative * (1.0 - identity)
    derivative = derivative - identity * derivative.sum(axis=1)[:, None]
    along_x = np.kron(np.kron(derivative, identity), identity)
    along_y = np.kron(np.kron(identity, derivative), identity)
    along_z = np.kron(identity, np.kron(identity, derivative))
    stacked = np.concatenate([along_x.T, along_y.T, along_z.T], axis=1)
    quad = np.array(GLL_WEIGHTS)
    cube = np.kron(np.kron(quad, quad), quad)
    return (jnp.asarray(stacked, dtype=jnp.float32), jnp.asarray(np.concatenate([cube, cube, cube]), dtype=jnp.float32))

def operate(fields, connect_parts, metric_parts, source_parts, stacked, weights):

    def one_part(items):
        values, links, scaled_metric, source = items
        element_vals = values[:, links]
        grads = jnp.dot(element_vals.reshape(-1, element_vals.shape[2]), stacked, precision=lax.Precision.HIGHEST, preferred_element_type=jnp.float32)
        flux = grads.reshape(2, links.shape[0], -1) * scaled_metric[None]
        back = jnp.dot(flux.reshape(-1, flux.shape[2]), stacked.T, precision=lax.Precision.HIGHEST, preferred_element_type=jnp.float32).reshape(element_vals.shape)
        residual = jnp.stack([source - back[0], -back[1]])
        return jax.ops.segment_sum(residual.reshape(2, -1).T, links.reshape(-1), num_segments=values.shape[1]).T
    return lax.map(one_part, (jnp.swapaxes(fields, 0, 1), connect_parts, metric_parts, source_parts))

def share_sums(local, shared):
    npart = local.shape[0]
    nodes = local.shape[2]
    padded = jnp.concatenate([jnp.swapaxes(local, 1, 2), jnp.zeros((npart, 1, 2), jnp.float32)], axis=1)
    part_ids = jnp.arange(npart, dtype=jnp.int32)
    dom_of = part_ids // N_SUB
    sub_of = part_ids % N_SUB
    offsets = jnp.arange(3, dtype=jnp.int32)
    peer_dom = jnp.clip(dom_of[:, None, None] + offsets[None, :, None] - 1, 0, N_DOM - 1)
    peer = peer_dom * N_SUB + jnp.arange(N_SUB, dtype=jnp.int32)[None, None, :]
    peer_list = shared[peer, (2 - offsets)[None, :, None], sub_of[:, None, None]]
    received = padded[peer[..., None], peer_list]
    summed = padded.at[part_ids[:, None, None, None], shared].add(received)
    return jnp.swapaxes(summed[:, :nodes], 1, 2)

def reference(field_prev, field_now, adjoint_now, adjoint_next, inv_mass, metric, connect, surface, driver, shared, filter_taps, signal):
    stacked, weights = element_tables()
    npart = field_now.shape[0]
    per_part = connect.shape[0] // npart
    connect_parts = connect.reshape(npart, per_part, -1)
    metric_parts = (metric * weights[None, :]).reshape(npart, per_part, -1)
    drive = jnp.dot(filter_taps, signal.T, precision=lax.Precision.HIGHEST, preferred_element_type=jnp.float32)
    onehot = (driver[:, None] == jnp.arange(DRIVERS, dtype=jnp.int32)[None, :]).astype(jnp.float32)
    scale = 1.0 / math.sqrt(ELEM_NODES * ELEMS)
    previous = jnp.stack([field_prev, adjoint_next])
    current = jnp.stack([field_now, adjoint_now])
    part_ids = jnp.arange(npart, dtype=jnp.int32)
    columns = []
    for step in range(STEPS):
        adjoint_vals = current[1][part_ids[:, None, None], connect_parts].reshape(-1, ELEM_NODES)
        products = lax.optimization_barrier(jnp.sum(surface * adjoint_vals, axis=1))
        columns.append(scale * lax.optimization_barrier(jnp.sum(onehot * products[:, None], axis=0)))
        amplitude = lax.optimization_barrier(jnp.sum(onehot * drive[:, step][None, :], axis=1))
        source = (amplitude[:, None] * surface).reshape(npart, per_part, -1)
        local = operate(current, connect_parts, metric_parts, source, stacked, weights)
        total = jnp.swapaxes(share_sums(local, shared), 0, 1)
        advanced = 2.0 * current - previous + inv_mass[None] * total
        previous = current
        current = advanced
    coefficients = jnp.stack(columns[::-1], axis=1)
    filter_grad = jnp.dot(coefficients, signal, precision=lax.Precision.HIGHEST, preferred_element_type=jnp.float32)
    return (current[0], current[1], filter_grad)
```

```python
import functools
import math

import jax
import jax.numpy as jnp
import numpy as np
from jax import lax
from jax.experimental import pallas as pl
from jax.experimental.pallas import tpu as pltpu
from jax.sharding import PartitionSpec as P

NN = 512
LANES = 128
ROWS = 64
COLS = 256
BLOCK = 8
ALL = ("dom", "sub", "chip")

GLL_POINTS = (
    -1.0,
    -0.8717401485096066,
    -0.5917001814331423,
    -0.2092992179024789,
    0.2092992179024789,
    0.5917001814331423,
    0.8717401485096066,
    1.0,
)
GLL_WEIGHTS = (
    0.03571428571428571,
    0.21070422714350603,
    0.3411226924835044,
    0.4124587946587038,
    0.4124587946587038,
    0.3411226924835044,
    0.21070422714350603,
    0.03571428571428571,
)
BF = jnp.bfloat16
F32 = jnp.float32


def element_tables():
    points = np.array(GLL_POINTS)
    identity = np.eye(8)
    diffs = points[:, None] - points[None, :] + identity
    barycentric = 1.0 / np.prod(diffs, axis=1)
    derivative = barycentric[None, :] / barycentric[:, None] / diffs
    derivative = derivative * (1.0 - identity)
    derivative = derivative - identity * derivative.sum(axis=1)[:, None]
    along_x = np.kron(derivative, np.eye(64)).T
    along_y = np.kron(np.eye(4), np.kron(derivative, identity)).T
    along_z = np.kron(np.eye(32), derivative).T
    quad = np.array(GLL_WEIGHTS)
    cube = np.kron(np.kron(quad, quad), quad)

    def parts(table):
        table = table.astype(np.float32)
        high = table.astype(jnp.bfloat16)
        low = (table - high.astype(np.float32)).astype(jnp.bfloat16)
        return high, low

    forward = []
    backward = []
    for table in (along_x, along_y, along_z):
        forward += parts(table)
        backward += parts(table.T)
    return forward, backward, np.concatenate([cube] * 3).astype(np.float32)[None, :]


def halves(x):
    high = x.astype(BF)
    return high, (x - high.astype(F32)).astype(BF)


def mm(a, b):
    return jnp.dot(a, b, preferred_element_type=F32)


def times(x, high, low):
    xh, xl = halves(x)
    rows = x.shape[0]
    both = mm(jnp.concatenate([xh, xl], axis=0), high)
    return both[:rows] + both[rows:] + mm(xh, low)


def stack_halves(x):
    return jnp.concatenate([x[:, :256], x[:, 256:]], axis=0)


def unstack_halves(x):
    rows = x.shape[0] // 2
    return jnp.concatenate([x[:rows], x[rows:]], axis=1)


def split_index(index):
    row = (index >> 7) & (ROWS - 1)
    column = (index & (LANES - 1)) | ((index >> 13) << 7)
    return row, column


def column_hot(column):
    ids = lax.broadcasted_iota(jnp.int32, (COLS, NN), 0).astype(BF)
    return jnp.where(ids == column.astype(BF), BF(1), BF(0))


def fill_table(table_ref, fields):
    for k in range(2):
        field = fields[k]
        plane = jnp.concatenate([field[:ROWS], field[ROWS:]], axis=1)
        high, low = halves(plane)
        table_ref[k * ROWS : (k + 1) * ROWS] = high
        table_ref[(2 + k) * ROWS : (3 + k) * ROWS] = low


def look_up(table, index):
    row, column = split_index(index)
    found = mm(table, column_hot(column))
    found = found[: 2 * ROWS] + found[2 * ROWS :]
    mask = lax.broadcasted_iota(jnp.int32, (ROWS, NN), 0) == row
    return [
        jnp.sum(jnp.where(mask, found[k * ROWS : (k + 1) * ROWS], 0.0), axis=0, keepdims=True)
        for k in range(2)
    ]


def spread(indices, values):
    columns = []
    placed = []
    ids = lax.broadcasted_iota(jnp.int32, (ROWS, NN), 0).astype(BF)
    for index, pair in zip(indices, values):
        row, column = split_index(index)
        columns.append(column_hot(column))
        mask = ids == row.astype(BF)
        terms = [halves(v) for v in pair]
        placed.append(
            jnp.concatenate(
                [jnp.where(mask, terms[k][s], BF(0)) for s in range(2) for k in range(2)], axis=0
            )
        )
    left = jnp.concatenate(placed, axis=1) if len(placed) > 1 else placed[0]
    right = jnp.concatenate(columns, axis=1) if len(columns) > 1 else columns[0]
    return lax.dot_general(left, right, (((1,), (1,)), ((), ())), preferred_element_type=F32)


def to_fields(sums):
    sums = sums[: 2 * ROWS] + sums[2 * ROWS :]
    return [
        jnp.concatenate(
            [
                sums[k * ROWS : (k + 1) * ROWS, :LANES],
                sums[k * ROWS : (k + 1) * ROWS, LANES:],
            ],
            axis=0,
        )
        for k in range(2)
    ]


def gather_all(table_ref, connect_ref, vals_ref):
    count = connect_ref.shape[0]
    table = table_ref[...]

    def body(i, carry):
        for u in range(BLOCK):
            e = i * BLOCK + u
            pair = look_up(table, connect_ref[pl.ds(e, 1), :])
            for k in range(2):
                vals_ref[k, pl.ds(e, 1), :] = pair[k]
        return carry

    lax.fori_loop(0, count // BLOCK, body, 0)


def operator(vals_ref, metric_ref, weights_ref, forward, backward, back_ref):
    count = vals_ref.shape[1]
    vals = jnp.concatenate([vals_ref[0], vals_ref[1]], axis=0)
    stacked = stack_halves(vals)
    total = None
    for i in range(3):
        scale = metric_ref[:, i * NN : (i + 1) * NN] * weights_ref[:, i * NN : (i + 1) * NN]
        scale = jnp.concatenate([scale, scale], axis=0)
        fh, fl = forward[2 * i][...], forward[2 * i + 1][...]
        bh, bl = backward[2 * i][...], backward[2 * i + 1][...]
        if i == 0:
            part = times(times(vals, fh, fl) * scale, bh, bl)
        else:
            grads = times(stacked, fh, fl) * stack_halves(scale)
            part = unstack_halves(times(grads, bh, bl))
        total = part if total is None else total + part
    back_ref[0] = total[:count]
    back_ref[1] = total[count:]


def driver_hot(driver_ref):
    count = driver_ref.shape[1]
    return (lax.broadcasted_iota(jnp.int32, (8, count), 0) == driver_ref[...]).astype(F32)


def driver_sums(vals_ref, surface_ref, driver_ref):
    products = surface_ref[...] * vals_ref[1]
    products = sum(products[:, i * LANES : (i + 1) * LANES] for i in range(NN // LANES))
    return jnp.dot(
        driver_hot(driver_ref),
        products,
        precision=lax.Precision.HIGHEST,
        preferred_element_type=F32,
    )


def add_source(step, drive_ref, surface_ref, driver_ref, back_ref):
    terms = drive_ref[...]
    terms = jnp.sum(terms[:, 8 * step : 8 * step + 8, :], axis=0)
    drive = jnp.broadcast_to(jnp.sum(terms, axis=1, keepdims=True), (8, LANES))
    amplitude = lax.dot_general(
        driver_hot(driver_ref),
        drive,
        (((0,), (0,)), ((), ())),
        precision=lax.Precision.HIGHEST,
        preferred_element_type=F32,
    )
    amplitude = jnp.concatenate([amplitude] * (NN // LANES), axis=1)
    back_ref[0] = amplitude * surface_ref[...] - back_ref[0]
    back_ref[1] = -back_ref[1]


def scatter_all(res_ref, connect_ref, sums_ref):
    count = connect_ref.shape[0]
    sums_ref[...] = jnp.zeros_like(sums_ref)

    def body(i, carry):
        rows = [pl.ds(i * BLOCK + u, 1) for u in range(BLOCK)]
        sums_ref[...] += spread(
            [connect_ref[r, :] for r in rows],
            [[res_ref[k, r, :] for k in range(2)] for r in rows],
        )
        return carry

    lax.fori_loop(0, count // BLOCK, body, 0)


def fill_send(where_ref, table_ref, shared_ref, partial, send_ref, *, doms, peers):
    table = table_ref[...]
    send_ref[:, :8, :] = jnp.zeros((send_ref.shape[0], 8, LANES), F32)
    for q in range(send_ref.shape[0]):
        send_ref[q, 8:, :] = partial
    for o in range(3):
        dom = where_ref[0] + (o - 1)
        for j in range(peers):
            slot = o * peers + j
            pair = look_up(table, shared_ref[slot : slot + 1, :])

            @pl.when((dom >= 0) & (dom < doms))
            def _():
                for chip in range(2):
                    to = (dom * peers + j) * 2 + chip
                    for k in range(2):
                        for i in range(4):
                            send_ref[pl.ds(to, 1), 4 * k + i, :] = pair[k][
                                :, i * LANES : (i + 1) * LANES
                            ]


def received_sums(where_ref, shared_ref, recv_ref, *, doms, peers):
    indices = []
    values = []
    for o in range(3):
        dom = jnp.clip(where_ref[0] + (o - 1), 0, doms - 1)
        for j in range(peers):
            slot = o * peers + j
            start = (dom * peers + j) * 2
            both = recv_ref[start, :8, :] + recv_ref[start + 1, :8, :]
            indices.append(shared_ref[slot : slot + 1, :])
            values.append(
                [
                    jnp.concatenate([both[4 * k + i : 4 * k + i + 1] for i in range(4)], axis=1)
                    for k in range(2)
                ]
            )
    total = None
    for at in range(0, len(indices), BLOCK):
        part = spread(indices[at : at + BLOCK], values[at : at + BLOCK])
        total = part if total is None else total + part
    return to_fields(total)


def advance(current, previous, mass_ref, own_ref, other_ref, received):
    return [
        2.0 * current[k] - previous[k] + mass_ref[...] * (own_ref[k] + other_ref[k] + received[k])
        for k in range(2)
    ]


def first_kernel(now0, now1, connect, surface, driver, metric, weights, *refs):
    tables, (back, partial, vals, table) = refs[:12], refs[12:]
    fill_table(table, [now0[...], now1[...]])
    gather_all(table, connect, vals)
    partial[...] = driver_sums(vals, surface, driver)
    operator(vals, metric, weights, tables[:6], tables[6:], back)


def local_sums(where, res, connect, shared, partial, local, send, sums, table, sizes):
    scatter_all(res, connect, sums)
    fields = to_fields(sums[...])
    for k in range(2):
        local[k] = fields[k]
    fill_table(table, fields)
    fill_send(where, table, shared, partial, send, **sizes)


def second_kernel(
    where, back, partial, drive, connect, surface, driver, shared, local, send, res, sums, table, *, sizes
):
    for k in range(2):
        res[k] = back[k]
    add_source(0, drive, surface, driver, res)
    local_sums(where, res, connect, shared, partial[...], local, send, sums, table, sizes)


def third_kernel(
    where,
    now0,
    now1,
    prev0,
    prev1,
    mass,
    own,
    other,
    recv,
    drive,
    connect,
    surface,
    driver,
    shared,
    metric,
    weights,
    *refs,
    sizes,
):
    tables, (current, local, send, vals, res, sums, table) = refs[:12], refs[12:]
    received = received_sums(where, shared, recv, **sizes)
    fields = advance(
        [now0[...], now1[...]], [prev0[...], prev1[...]], mass, own, other, received
    )
    for k in range(2):
        current[k] = fields[k]
    fill_table(table, fields)
    gather_all(table, connect, vals)
    partial = driver_sums(vals, surface, driver)
    operator(vals, metric, weights, tables[:6], tables[6:], res)
    add_source(1, drive, surface, driver, res)
    local_sums(where, res, connect, shared, partial, local, send, sums, table, sizes)


def last_kernel(
    where, current, now0, now1, mass, own, other, recv_before, recv, shared, signal, out0, out1, grad, *, sizes, scale
):
    received = received_sums(where, shared, recv, **sizes)
    fields = advance(
        [current[0], current[1]], [now0[...], now1[...]], mass, own, other, received
    )
    out0[...] = fields[0]
    out1[...] = fields[1]

    def column(ref):
        return jnp.sum(jnp.sum(ref[:, 8:, :], axis=0), axis=1, keepdims=True) * scale

    grad[...] = column(recv) * signal[0:1, :] + column(recv_before) * signal[1:2, :]


VMEM = pl.BlockSpec(memory_space=pltpu.VMEM)
SMEM = pl.BlockSpec(memory_space=pltpu.SMEM)


def call(body, name, scalars, arrays, outs, scratch):
    return pl.pallas_call(
        body,
        out_shape=[jax.ShapeDtypeStruct(shape, F32) for shape in outs],
        in_specs=[SMEM] * len(scalars) + [VMEM] * len(arrays),
        out_specs=[VMEM] * len(outs),
        scratch_shapes=[pltpu.VMEM(shape, dtype) for shape, dtype in scratch],
        compiler_params=pltpu.CompilerParams(vmem_limit_bytes=56 << 20),
        name=name,
    )(*scalars, *arrays)


def on_device(
    field_prev,
    field_now,
    adjoint_now,
    adjoint_next,
    inv_mass,
    metric,
    connect,
    surface,
    driver,
    shared,
    filter_taps,
    signal,
):
    forward, backward, weights = element_tables()
    tables = [jnp.asarray(t) for t in forward + backward]
    count = connect.shape[0]
    peers = shared.shape[2]
    doms = lax.axis_size("dom")
    devices = lax.axis_size(ALL)
    width = filter_taps.shape[1]
    sizes = dict(doms=doms, peers=peers)
    where = lax.axis_index("dom").astype(jnp.int32).reshape(1)
    plane = (LANES, LANES)
    now0, now1, prev0, prev1, mass = (
        x.reshape(plane) for x in (field_now, adjoint_now, field_prev, adjoint_next, inv_mass)
    )
    links = shared.reshape(3 * peers, NN)
    driver_row = driver.reshape(1, count)
    own_signal = lax.dynamic_slice_in_dim(signal, lax.axis_index(ALL) * width, width, 1)
    terms = (own_signal[:, None, :] * filter_taps[None]).reshape(16, width)
    if width > LANES:
        terms = jnp.sum(terms, axis=1, keepdims=True)
    terms = jnp.pad(terms, ((0, 0), (0, LANES - terms.shape[1])))
    terms = jnp.broadcast_to(terms[None], (devices, 16, LANES))

    def trade(x):
        return lax.all_to_all(x, ALL, 0, 0, tiled=True)

    def swap(x):
        return lax.ppermute(x, "chip", [(0, 1), (1, 0)])

    drive = trade(terms)
    nodes = ((2,) + plane, F32)
    elements = ((2, count, NN), F32)
    sums = ((4 * ROWS, COLS), F32)
    table = ((4 * ROWS, COLS), BF)
    packet = (devices, 16, LANES)
    back, partial = call(
        first_kernel,
        "operator0",
        [],
        [now0, now1, connect, surface, driver_row, metric, jnp.asarray(weights)] + tables,
        [elements[0], (8, LANES)],
        [elements, table],
    )
    local, send = call(
        functools.partial(second_kernel, sizes=sizes),
        "assemble0",
        [where],
        [back, partial, drive, connect, surface, driver_row, links],
        [nodes[0], packet],
        [elements, sums, table],
    )
    other = swap(local)
    recv0 = trade(send)
    current, local, send = call(
        functools.partial(third_kernel, sizes=sizes),
        "step1",
        [where],
        [now0, now1, prev0, prev1, mass, local, other, recv0, drive, connect, surface, driver_row, links]
        + [metric, jnp.asarray(weights)]
        + tables,
        [nodes[0], nodes[0], packet],
        [elements, elements, sums, table],
    )
    other = swap(local)
    recv1 = trade(send)
    out0, out1, grad = call(
        functools.partial(
            last_kernel, sizes=sizes, scale=1.0 / math.sqrt(NN * count * devices)
        ),
        "finish",
        [where],
        [current, now0, now1, mass, local, other, recv0, recv1, links, own_signal],
        [plane, plane, (8, width)],
        [],
    )
    return out0.reshape(1, -1), out1.reshape(1, -1), grad


def solution(mesh):
    region = P(("groups", "dom", "sub"), None)
    element = P(("groups", "dom", "sub", "chip"), None)
    in_specs = (
        region,
        region,
        region,
        region,
        region,
        element,
        element,
        element,
        P(("groups", "dom", "sub", "chip")),
        P(("groups", "dom", "sub"), None, None, None),
        P(None, ALL),
        P(),
    )
    out_specs = (region, region, P("groups", ALL))
    return jax.shard_map(
        on_device, mesh=mesh, in_specs=in_specs, out_specs=out_specs, check_vma=False
    )
```

```python
import functools
import math

import jax
import jax.numpy as jnp
import numpy as np
from jax import lax
from jax.experimental import pallas as pl
from jax.experimental.pallas import tpu as pltpu
from jax.sharding import PartitionSpec as P

NN = 512
LANES = 128
ROWS = 64
COLS = 256
BLOCK = 64
PACKET = 2 * NN + LANES
ALL = ("dom", "sub", "chip")

GLL_POINTS = (
    -1.0,
    -0.8717401485096066,
    -0.5917001814331423,
    -0.2092992179024789,
    0.2092992179024789,
    0.5917001814331423,
    0.8717401485096066,
    1.0,
)
GLL_WEIGHTS = (
    0.03571428571428571,
    0.21070422714350603,
    0.3411226924835044,
    0.4124587946587038,
    0.4124587946587038,
    0.3411226924835044,
    0.21070422714350603,
    0.03571428571428571,
)
BF = jnp.bfloat16
F32 = jnp.float32


def element_tables():
    points = np.array(GLL_POINTS)
    identity = np.eye(8)
    diffs = points[:, None] - points[None, :] + identity
    barycentric = 1.0 / np.prod(diffs, axis=1)
    derivative = barycentric[None, :] / barycentric[:, None] / diffs
    derivative = derivative * (1.0 - identity)
    derivative = derivative - identity * derivative.sum(axis=1)[:, None]
    along_x = np.kron(derivative, np.eye(64)).T
    along_y = np.kron(np.eye(4), np.kron(derivative, identity)).T
    along_z = np.kron(np.eye(32), derivative).T
    quad = np.array(GLL_WEIGHTS)
    cube = np.kron(np.kron(quad, quad), quad)

    def parts(table):
        table = table.astype(np.float32)
        high = table.astype(jnp.bfloat16)
        low = (table - high.astype(np.float32)).astype(jnp.bfloat16)
        return high, low

    forward = []
    backward = []
    for table in (along_x, along_y, along_z):
        forward += parts(table)
        backward += parts(table.T)
    return forward, backward, np.concatenate([cube] * 3).astype(np.float32)[None, :]


def halves(x):
    high = x.astype(BF)
    return high, (x - high.astype(F32)).astype(BF)


def mm(a, b):
    return jnp.dot(a, b, preferred_element_type=F32)


def times(x, high, low):
    xh, xl = halves(x)
    rows = x.shape[0]
    both = mm(jnp.concatenate([xh, xl], axis=0), high)
    return both[:rows] + both[rows:] + mm(xh, low)


def stack_halves(x):
    return jnp.concatenate([x[:, :256], x[:, 256:]], axis=0)


def unstack_halves(x):
    rows = x.shape[0] // 2
    return jnp.concatenate([x[:rows], x[rows:]], axis=1)


def split_index(index):
    row = (index >> 7) & (ROWS - 1)
    column = (index & (LANES - 1)) | ((index >> 13) << 7)
    return row, column


def column_hot(column):
    ids = lax.broadcasted_iota(jnp.int32, (COLS, NN), 0).astype(BF)
    return jnp.where(ids == column.astype(BF), BF(1), BF(0))


def fill_table(table_ref, fields):
    for k in range(2):
        field = fields[k]
        plane = jnp.concatenate([field[:ROWS], field[ROWS:]], axis=1)
        high, low = halves(plane)
        table_ref[k * ROWS : (k + 1) * ROWS] = high
        table_ref[(2 + k) * ROWS : (3 + k) * ROWS] = low


def look_up(table, index):
    row, column = split_index(index)
    found = mm(table, column_hot(column))
    found = found[: 2 * ROWS] + found[2 * ROWS :]
    mask = lax.broadcasted_iota(jnp.int32, (ROWS, NN), 0) == row
    return [
        jnp.sum(jnp.where(mask, found[k * ROWS : (k + 1) * ROWS], 0.0), axis=0, keepdims=True)
        for k in range(2)
    ]


def spread(indices, values):
    columns = []
    placed = []
    ids = lax.broadcasted_iota(jnp.int32, (ROWS, NN), 0).astype(BF)
    for index, pair in zip(indices, values):
        row, column = split_index(index)
        columns.append(column_hot(column))
        mask = ids == row.astype(BF)
        terms = [halves(v) for v in pair]
        placed.append(
            jnp.concatenate(
                [jnp.where(mask, terms[k][s], BF(0)) for s in range(2) for k in range(2)], axis=0
            )
        )
    left = jnp.concatenate(placed, axis=1) if len(placed) > 1 else placed[0]
    right = jnp.concatenate(columns, axis=1) if len(columns) > 1 else columns[0]
    return lax.dot_general(left, right, (((1,), (1,)), ((), ())), preferred_element_type=F32)


def to_fields(sums):
    sums = sums[: 2 * ROWS] + sums[2 * ROWS :]
    return [
        jnp.concatenate(
            [
                sums[k * ROWS : (k + 1) * ROWS, :LANES],
                sums[k * ROWS : (k + 1) * ROWS, LANES:],
            ],
            axis=0,
        )
        for k in range(2)
    ]


def gather_all(table_ref, connect_ref, vals_ref):
    count = connect_ref.shape[0]
    table = table_ref[...]

    def body(i, carry):
        for u in range(BLOCK):
            e = i * BLOCK + u
            pair = look_up(table, connect_ref[pl.ds(e, 1), :])
            for k in range(2):
                vals_ref[k, pl.ds(e, 1), :] = pair[k]
        return carry

    if count == BLOCK:
        body(0, 0)
    else:
        lax.fori_loop(0, count // BLOCK, body, 0)


def operator(vals_ref, metric_ref, weights_ref, forward, backward, back_ref):
    count = vals_ref.shape[1]
    vals = jnp.concatenate([vals_ref[0], vals_ref[1]], axis=0)
    stacked = stack_halves(vals)
    total = None
    for i in range(3):
        scale = metric_ref[:, i * NN : (i + 1) * NN] * weights_ref[:, i * NN : (i + 1) * NN]
        scale = jnp.concatenate([scale, scale], axis=0)
        fh, fl = forward[2 * i][...], forward[2 * i + 1][...]
        bh, bl = backward[2 * i][...], backward[2 * i + 1][...]
        if i == 0:
            part = times(times(vals, fh, fl) * scale, bh, bl)
        else:
            grads = times(stacked, fh, fl) * stack_halves(scale)
            part = unstack_halves(times(grads, bh, bl))
        total = part if total is None else total + part
    back_ref[0] = total[:count]
    back_ref[1] = total[count:]


def driver_hot(driver_ref):
    count = driver_ref.shape[1]
    return (lax.broadcasted_iota(jnp.int32, (8, count), 0) == driver_ref[...]).astype(F32)


def driver_sums(vals_ref, surface_ref, driver_ref):
    products = surface_ref[...] * vals_ref[1]
    products = sum(products[:, i * LANES : (i + 1) * LANES] for i in range(NN // LANES))
    lanes = (((1,), (1,)), ((), ()))
    per_element = lax.dot_general(
        jnp.ones((8, LANES), F32),
        products,
        lanes,
        precision=lax.Precision.HIGHEST,
        preferred_element_type=F32,
    )
    count = driver_ref.shape[1]
    hot = lax.broadcasted_iota(jnp.int32, (LANES, count), 0) == driver_ref[...]
    hot = (hot & (lax.broadcasted_iota(jnp.int32, (LANES, count), 0) < 8)).astype(F32)
    return lax.dot_general(
        per_element, hot, lanes, precision=lax.Precision.HIGHEST, preferred_element_type=F32
    )[:1]


def add_source(step, drive_ref, surface_ref, driver_ref, back_ref):
    terms = jnp.sum(drive_ref[...], axis=0)
    half = lax.broadcasted_iota(jnp.int32, (8, LANES), 1) >> 6
    terms = jnp.where(half == step, terms, 0.0)
    drive = jnp.broadcast_to(jnp.sum(terms, axis=1, keepdims=True), (8, LANES))
    amplitude = lax.dot_general(
        driver_hot(driver_ref),
        drive,
        (((0,), (0,)), ((), ())),
        precision=lax.Precision.HIGHEST,
        preferred_element_type=F32,
    )
    amplitude = jnp.concatenate([amplitude] * (NN // LANES), axis=1)
    back_ref[0] = amplitude * surface_ref[...] - back_ref[0]
    back_ref[1] = -back_ref[1]


def scatter_all(res_ref, connect_ref, sums_ref):
    count = connect_ref.shape[0]

    def part(i):
        rows = [pl.ds(i * BLOCK + u, 1) for u in range(BLOCK)]
        return spread(
            [connect_ref[r, :] for r in rows],
            [[res_ref[k, r, :] for k in range(2)] for r in rows],
        )

    if count == BLOCK:
        sums_ref[...] = part(0)
        return
    sums_ref[...] = jnp.zeros_like(sums_ref)

    def body(i, carry):
        sums_ref[...] += part(i)
        return carry

    lax.fori_loop(0, count // BLOCK, body, 0)


def fill_send(where_ref, table_ref, shared_ref, partial, send_ref, *, doms, peers):
    table = table_ref[...]
    empty = jnp.concatenate([jnp.zeros((1, 2 * NN), F32), partial], axis=1)
    for q in range(send_ref.shape[0]):
        send_ref[q] = empty
    for o in range(3):
        dom = where_ref[0] + (o - 1)
        for j in range(peers):
            pair = look_up(table, shared_ref[o, j : j + 1, :])
            values = jnp.concatenate(pair, axis=1)

            @pl.when((dom >= 0) & (dom < doms))
            def _():
                for chip in range(2):
                    send_ref[(dom * peers + j) * 2 + chip, :, : 2 * NN] = values


def received_sums(where_ref, shared_ref, recv_ref, *, doms, peers):
    indices = []
    values = []
    for o in range(3):
        dom = jnp.clip(where_ref[0] + (o - 1), 0, doms - 1)
        for j in range(peers):
            start = (dom * peers + j) * 2
            both = recv_ref[start] + recv_ref[start + 1]
            indices.append(shared_ref[o, j : j + 1, :])
            values.append([both[:, k * NN : (k + 1) * NN] for k in range(2)])
    total = None
    for at in range(0, len(indices), 8):
        part = spread(indices[at : at + 8], values[at : at + 8])
        total = part if total is None else total + part
    return to_fields(total)


def advance(current, previous, mass_ref, own_ref, other_ref, received):
    return [
        2.0 * current[k] - previous[k] + mass_ref[...] * (own_ref[k] + other_ref[k] + received[k])
        for k in range(2)
    ]


def drive_kernel(taps, signal, send):
    folded = []
    for t in range(2):
        products = taps[...] * signal[t : t + 1, :]
        products = sum(
            products[:, i * LANES : (i + 1) * LANES] for i in range(products.shape[1] // LANES)
        )
        folded.append(products[:, :64] + products[:, 64:])
    terms = jnp.concatenate(folded, axis=1)
    for q in range(send.shape[0]):
        send[q] = terms


def first_kernel(now0, now1, connect, surface, driver, metric, weights, *refs):
    tables, (back, partial, vals, table) = refs[:12], refs[12:]
    fill_table(table, [now0[...], now1[...]])
    gather_all(table, connect, vals)
    partial[...] = driver_sums(vals, surface, driver)
    operator(vals, metric, weights, tables[:6], tables[6:], back)


def local_sums(where, res, connect, shared, partial, local, send, sums, table, sizes):
    scatter_all(res, connect, sums)
    fields = to_fields(sums[...])
    for k in range(2):
        local[k] = fields[k]
    fill_table(table, fields)
    fill_send(where, table, shared, partial, send, **sizes)


def second_kernel(
    where, back, partial, drive, connect, surface, driver, shared, local, send, res, sums, table, *, sizes
):
    for k in range(2):
        res[k] = back[k]
    add_source(0, drive, surface, driver, res)
    local_sums(where, res, connect, shared, partial[...], local, send, sums, table, sizes)


def third_kernel(
    where,
    now0,
    now1,
    prev0,
    prev1,
    mass,
    own,
    other,
    recv,
    drive,
    connect,
    surface,
    driver,
    shared,
    metric,
    weights,
    *refs,
    sizes,
):
    tables, (current, local, send, vals, res, sums, table) = refs[:12], refs[12:]
    received = received_sums(where, shared, recv, **sizes)
    fields = advance(
        [now0[...], now1[...]], [prev0[...], prev1[...]], mass, own, other, received
    )
    for k in range(2):
        current[k] = fields[k]
    fill_table(table, fields)
    gather_all(table, connect, vals)
    partial = driver_sums(vals, surface, driver)
    operator(vals, metric, weights, tables[:6], tables[6:], res)
    add_source(1, drive, surface, driver, res)
    local_sums(where, res, connect, shared, partial, local, send, sums, table, sizes)


def last_kernel(
    where, current, now0, now1, mass, own, other, recv_before, recv, shared, signal, out0, out1, grad, *, sizes, scale
):
    received = received_sums(where, shared, recv, **sizes)
    fields = advance(
        [current[0], current[1]], [now0[...], now1[...]], mass, own, other, received
    )
    out0[...] = fields[0]
    out1[...] = fields[1]

    def column(ref):
        row = sum(ref[q, :, 2 * NN :] for q in range(ref.shape[0]))
        ids = [lax.broadcasted_iota(jnp.int32, (8, LANES), axis) for axis in range(2)]
        row = jnp.where(ids[0] == ids[1], jnp.broadcast_to(row, (8, LANES)), 0.0)
        return jnp.sum(row, axis=1, keepdims=True) * scale

    grad[...] = column(recv) * signal[0:1, :] + column(recv_before) * signal[1:2, :]


VMEM = pl.BlockSpec(memory_space=pltpu.VMEM)
SMEM = pl.BlockSpec(memory_space=pltpu.SMEM)


def call(body, name, scalars, arrays, outs, scratch):
    return pl.pallas_call(
        body,
        out_shape=[jax.ShapeDtypeStruct(shape, F32) for shape in outs],
        in_specs=[SMEM] * len(scalars) + [VMEM] * len(arrays),
        out_specs=[VMEM] * len(outs),
        scratch_shapes=[pltpu.VMEM(shape, dtype) for shape, dtype in scratch],
        compiler_params=pltpu.CompilerParams(vmem_limit_bytes=56 << 20),
        name=name,
    )(*scalars, *arrays)


def on_device(
    field_prev,
    field_now,
    adjoint_now,
    adjoint_next,
    inv_mass,
    metric,
    connect,
    surface,
    driver,
    shared,
    filter_taps,
    signal,
):
    forward, backward, weights = element_tables()
    tables = [jnp.asarray(t) for t in forward + backward]
    count = connect.shape[0]
    peers = shared.shape[2]
    doms = lax.axis_size("dom")
    devices = lax.axis_size(ALL)
    width = filter_taps.shape[1]
    sizes = dict(doms=doms, peers=peers)
    where = lax.axis_index("dom").astype(jnp.int32).reshape(1)
    plane = (LANES, LANES)
    now0, now1, prev0, prev1, mass = (
        x.reshape(plane) for x in (field_now, adjoint_now, field_prev, adjoint_next, inv_mass)
    )
    links = shared.reshape(3, peers, NN)
    driver_row = driver.reshape(1, count)
    own_signal = lax.dynamic_slice_in_dim(signal, lax.axis_index(ALL) * width, width, 1)
    def trade(x):
        return lax.all_to_all(x, ALL, 0, 0, tiled=True)

    def swap(x):
        return lax.ppermute(x, "chip", [(0, 1), (1, 0)])

    if width < LANES:
        pad = ((0, 0), (0, LANES - width))
        tap_block, signal_block = jnp.pad(filter_taps, pad), jnp.pad(own_signal, pad)
    else:
        tap_block, signal_block = filter_taps, own_signal
    (terms,) = call(
        drive_kernel, "drive", [], [tap_block, signal_block], [(devices, 8, LANES)], []
    )
    drive = trade(terms)
    nodes = ((2,) + plane, F32)
    elements = ((2, count, NN), F32)
    sums = ((4 * ROWS, COLS), F32)
    table = ((4 * ROWS, COLS), BF)
    packet = (devices, 1, PACKET)
    back, partial = call(
        first_kernel,
        "operator0",
        [],
        [now0, now1, connect, surface, driver_row, metric, jnp.asarray(weights)] + tables,
        [elements[0], (1, LANES)],
        [elements, table],
    )
    local, send = call(
        functools.partial(second_kernel, sizes=sizes),
        "assemble0",
        [where],
        [back, partial, drive, connect, surface, driver_row, links],
        [nodes[0], packet],
        [elements, sums, table],
    )
    other = swap(local)
    recv0 = trade(send)
    current, local, send = call(
        functools.partial(third_kernel, sizes=sizes),
        "step1",
        [where],
        [now0, now1, prev0, prev1, mass, local, other, recv0, drive, connect, surface, driver_row, links]
        + [metric, jnp.asarray(weights)]
        + tables,
        [nodes[0], nodes[0], packet],
        [elements, elements, sums, table],
    )
    other = swap(local)
    recv1 = trade(send)
    out0, out1, grad = call(
        functools.partial(
            last_kernel, sizes=sizes, scale=1.0 / math.sqrt(NN * count * devices)
        ),
        "finish",
        [where],
        [current, now0, now1, mass, local, other, recv0, recv1, links, own_signal],
        [plane, plane, (8, width)],
        [],
    )
    return out0.reshape(1, -1), out1.reshape(1, -1), grad


def solution(mesh):
    region = P(("groups", "dom", "sub"), None)
    element = P(("groups", "dom", "sub", "chip"), None)
    in_specs = (
        region,
        region,
        region,
        region,
        region,
        element,
        element,
        element,
        P(("groups", "dom", "sub", "chip")),
        P(("groups", "dom", "sub"), None, None, None),
        P(None, ALL),
        P(),
    )
    out_specs = (region, region, P("groups", ALL))
    return jax.shard_map(
        on_device, mesh=mesh, in_specs=in_specs, out_specs=out_specs, check_vma=False
    )
```

```python
import functools
import math

import jax
import jax.numpy as jnp
import numpy as np
from jax import lax
from jax.experimental import pallas as pl
from jax.experimental.pallas import tpu as pltpu
from jax.sharding import PartitionSpec as P

NN = 512
LANES = 128
ROWS = 64
COLS = 256
BLOCK = 32
PACKET = 2 * NN + LANES
ALL = ("dom", "sub", "chip")

GLL_POINTS = (
    -1.0,
    -0.8717401485096066,
    -0.5917001814331423,
    -0.2092992179024789,
    0.2092992179024789,
    0.5917001814331423,
    0.8717401485096066,
    1.0,
)
GLL_WEIGHTS = (
    0.03571428571428571,
    0.21070422714350603,
    0.3411226924835044,
    0.4124587946587038,
    0.4124587946587038,
    0.3411226924835044,
    0.21070422714350603,
    0.03571428571428571,
)
BF = jnp.bfloat16
F32 = jnp.float32


def element_tables():
    points = np.array(GLL_POINTS)
    identity = np.eye(8)
    diffs = points[:, None] - points[None, :] + identity
    barycentric = 1.0 / np.prod(diffs, axis=1)
    derivative = barycentric[None, :] / barycentric[:, None] / diffs
    derivative = derivative * (1.0 - identity)
    derivative = derivative - identity * derivative.sum(axis=1)[:, None]
    along_x = np.kron(derivative, np.eye(64)).T
    along_y = np.kron(np.eye(4), np.kron(derivative, identity)).T
    along_z = np.kron(np.eye(32), derivative).T
    quad = np.array(GLL_WEIGHTS)
    cube = np.kron(np.kron(quad, quad), quad)

    def parts(table):
        table = table.astype(np.float32)
        high = table.astype(jnp.bfloat16)
        low = (table - high.astype(np.float32)).astype(jnp.bfloat16)
        return high, low

    wide = list(parts(along_x)) + list(parts(along_x.T))
    narrow = []
    for table in (along_y, along_z, along_y.T, along_z.T):
        narrow += parts(table)
    weights = np.concatenate([cube] * 3).astype(np.float32)[None, :]
    return np.stack(wide), np.stack(narrow), weights


def halves(x):
    high = x.astype(BF)
    return high, (x - high.astype(F32)).astype(BF)


def mm(a, b):
    return jnp.dot(a, b, preferred_element_type=F32)


def times(x, high, low):
    xh, xl = halves(x)
    rows = x.shape[0]
    both = mm(jnp.concatenate([xh, xl], axis=0), high)
    return both[:rows] + both[rows:] + mm(xh, low)


def stack_halves(x):
    return jnp.concatenate([x[:, :256], x[:, 256:]], axis=0)


def unstack_halves(x):
    rows = x.shape[0] // 2
    return jnp.concatenate([x[:rows], x[rows:]], axis=1)


def split_index(index):
    row = (index >> 7) & (ROWS - 1)
    column = (index & (LANES - 1)) | ((index >> 13) << 7)
    return row, column


def column_hot(column):
    ids = lax.broadcasted_iota(jnp.int32, (COLS, NN), 0).astype(BF)
    return jnp.where(ids == column.astype(BF), BF(1), BF(0))


def fill_table(table_ref, fields):
    for k in range(2):
        field = fields[k]
        plane = jnp.concatenate([field[:ROWS], field[ROWS:]], axis=1)
        high, low = halves(plane)
        table_ref[k * ROWS : (k + 1) * ROWS] = high
        table_ref[(2 + k) * ROWS : (3 + k) * ROWS] = low


def look_up(table, index):
    row, column = split_index(index)
    found = mm(table, column_hot(column))
    found = found[: 2 * ROWS] + found[2 * ROWS :]
    mask = lax.broadcasted_iota(jnp.int32, (ROWS, NN), 0) == row
    return [
        jnp.sum(jnp.where(mask, found[k * ROWS : (k + 1) * ROWS], 0.0), axis=0, keepdims=True)
        for k in range(2)
    ]


def spread(indices, values):
    columns = []
    placed = []
    ids = lax.broadcasted_iota(jnp.int32, (ROWS, NN), 0).astype(BF)
    for index, pair in zip(indices, values):
        row, column = split_index(index)
        columns.append(column_hot(column))
        mask = ids == row.astype(BF)
        terms = [halves(v) for v in pair]
        placed.append(
            jnp.concatenate(
                [jnp.where(mask, terms[k][s], BF(0)) for s in range(2) for k in range(2)], axis=0
            )
        )
    left = jnp.concatenate(placed, axis=1) if len(placed) > 1 else placed[0]
    right = jnp.concatenate(columns, axis=1) if len(columns) > 1 else columns[0]
    return lax.dot_general(left, right, (((1,), (1,)), ((), ())), preferred_element_type=F32)


def to_fields(sums):
    sums = sums[: 2 * ROWS] + sums[2 * ROWS :]
    return [
        jnp.concatenate(
            [
                sums[k * ROWS : (k + 1) * ROWS, :LANES],
                sums[k * ROWS : (k + 1) * ROWS, LANES:],
            ],
            axis=0,
        )
        for k in range(2)
    ]


def gather_all(table_ref, connect_ref, vals_ref):
    count = connect_ref.shape[0]
    table = table_ref[...]

    def body(i, carry):
        for u in range(BLOCK):
            e = i * BLOCK + u
            pair = look_up(table, connect_ref[pl.ds(e, 1), :])
            for k in range(2):
                vals_ref[k, pl.ds(e, 1), :] = pair[k]
        return carry

    if count == BLOCK:
        body(0, 0)
    else:
        lax.fori_loop(0, count // BLOCK, body, 0)


def operator(vals_ref, metric, weights, wide, narrow, back_ref):
    count = vals_ref.shape[1]
    vals = jnp.concatenate([vals_ref[0], vals_ref[1]], axis=0)
    stacked = stack_halves(vals)
    metric_ref, weights_ref = metric(), weights()
    total = None
    for i in (1, 2, 0):
        scale = metric_ref[:, i * NN : (i + 1) * NN] * weights_ref[:, i * NN : (i + 1) * NN]
        scale = jnp.concatenate([scale, scale], axis=0)
        if i == 0:
            table = wide()
            part = times(times(vals, table[0], table[1]) * scale, table[2], table[3])
        else:
            table = narrow()
            at = 2 * (i - 1)
            grads = times(stacked, table[at], table[at + 1]) * stack_halves(scale)
            part = unstack_halves(times(grads, table[at + 4], table[at + 5]))
        total = part if total is None else total + part
    back_ref[0] = total[:count]
    back_ref[1] = total[count:]


def driver_hot(driver_ref):
    count = driver_ref.shape[1]
    return (lax.broadcasted_iota(jnp.int32, (8, count), 0) == driver_ref[...]).astype(F32)


def driver_sums(vals_ref, surface_ref, driver_ref):
    products = surface_ref[...] * vals_ref[1]
    products = sum(products[:, i * LANES : (i + 1) * LANES] for i in range(NN // LANES))
    lanes = (((1,), (1,)), ((), ()))
    per_element = lax.dot_general(
        jnp.ones((8, LANES), F32),
        products,
        lanes,
        precision=lax.Precision.HIGHEST,
        preferred_element_type=F32,
    )
    count = driver_ref.shape[1]
    hot = lax.broadcasted_iota(jnp.int32, (LANES, count), 0) == driver_ref[...]
    hot = (hot & (lax.broadcasted_iota(jnp.int32, (LANES, count), 0) < 8)).astype(F32)
    return lax.dot_general(
        per_element, hot, lanes, precision=lax.Precision.HIGHEST, preferred_element_type=F32
    )[:1]


def residual(step, drive_ref, surface_ref, driver_ref, back_ref, res_ref):
    terms = jnp.sum(drive_ref[...], axis=0)
    half = lax.broadcasted_iota(jnp.int32, (8, LANES), 1) >> 6
    terms = jnp.where(half == step, terms, 0.0)
    drive = jnp.broadcast_to(jnp.sum(terms, axis=1, keepdims=True), (8, LANES))
    amplitude = lax.dot_general(
        driver_hot(driver_ref),
        drive,
        (((0,), (0,)), ((), ())),
        precision=lax.Precision.HIGHEST,
        preferred_element_type=F32,
    )
    amplitude = jnp.concatenate([amplitude] * (NN // LANES), axis=1)
    res_ref[0] = amplitude * surface_ref[...] - back_ref[0]
    res_ref[1] = -back_ref[1]


def scatter_all(res_ref, connect_ref, sums_ref):
    count = connect_ref.shape[0]

    def part(i):
        rows = [pl.ds(i * BLOCK + u, 1) for u in range(BLOCK)]
        return spread(
            [connect_ref[r, :] for r in rows],
            [[res_ref[k, r, :] for k in range(2)] for r in rows],
        )

    if count == BLOCK:
        sums_ref[...] = part(0)
        return
    sums_ref[...] = jnp.zeros_like(sums_ref)

    def body(i, carry):
        sums_ref[...] += part(i)
        return carry

    lax.fori_loop(0, count // BLOCK, body, 0)


def fill_send(table_ref, shared_ref, partial, send_ref, *, doms, peers):
    table = table_ref[...]
    empty = jnp.concatenate([jnp.zeros((1, 2 * NN), F32), partial], axis=1)
    for q in range(send_ref.shape[0]):
        send_ref[q] = empty
    slots = [(o, j) for o in (0, 2, 1) for j in range(peers)]
    packets = [
        jnp.concatenate(look_up(table, shared_ref[o, j : j + 1, :]), axis=1) for o, j in slots
    ]
    for (o, j), packet in zip(slots, packets):
        dom = jnp.clip(lax.axis_index("dom") + (o - 1), 0, doms - 1)
        for chip in range(2):
            send_ref[(dom * peers + j) * 2 + chip, :, : 2 * NN] = packet


def received_sums(shared_ref, recv_ref, *, doms, peers):
    indices = []
    values = []
    for o in range(3):
        dom = jnp.clip(lax.axis_index("dom") + (o - 1), 0, doms - 1)
        for j in range(peers):
            start = (dom * peers + j) * 2
            both = recv_ref[start] + recv_ref[start + 1]
            indices.append(shared_ref[o, j : j + 1, :])
            values.append([both[:, k * NN : (k + 1) * NN] for k in range(2)])
    total = None
    for at in range(0, len(indices), 8):
        part = spread(indices[at : at + 8], values[at : at + 8])
        total = part if total is None else total + part
    return to_fields(total)


def advance(current, previous, mass, own, other, received):
    return [
        2.0 * current[k] - previous[k] + mass * (own[k] + other[k] + received[k]) for k in range(2)
    ]


def drive_kernel(ins, outs, scratch):
    taps, signal = (ref() for ref in ins)
    (send,) = outs
    folded = []
    for t in range(2):
        products = taps[...] * signal[t : t + 1, :]
        products = sum(
            products[:, i * LANES : (i + 1) * LANES] for i in range(products.shape[1] // LANES)
        )
        folded.append(products[:, :64] + products[:, 64:])
    terms = jnp.concatenate(folded, axis=1)
    for q in range(send.shape[0]):
        send[q] = terms


def first_kernel(ins, outs, scratch):
    connect, now0, now1, surface, driver, metric, weights, narrow, wide = ins
    back, partial = outs
    vals, table = scratch
    fill_table(table, [now0()[...], now1()[...]])
    gather_all(table, connect(), vals)
    partial[...] = driver_sums(vals, surface(), driver())
    operator(vals, metric, weights, wide, narrow, back)


def local_sums(res, connect, shared, partial, local, send, sums, table, sizes):
    scatter_all(res, connect, sums)
    fields = to_fields(sums[...])
    for k in range(2):
        local[k] = fields[k]
    local.flush()
    fill_table(table, fields)
    fill_send(table, shared, partial, send, **sizes)


def second_kernel(ins, outs, scratch, *, sizes):
    drive, surface, driver, back, connect, partial, shared = ins
    local, send = outs
    res, sums, table = scratch
    residual(0, drive(), surface(), driver(), back(), res)
    local_sums(res, connect(), shared(), partial()[...], local, send, sums, table, sizes)


def third_kernel(ins, outs, scratch, *, sizes):
    recv, shared, now0, now1, prev0, prev1, mass, own, other = ins[:9]
    connect, surface, driver, metric, weights, narrow, wide, drive = ins[9:]
    current, local, send = outs
    vals, back, res, sums, table = scratch
    received = received_sums(shared(), recv(), **sizes)
    fields = advance(
        [now0()[...], now1()[...]],
        [prev0()[...], prev1()[...]],
        mass()[...],
        own(),
        other(),
        received,
    )
    for k in range(2):
        current[k] = fields[k]
    current.flush()
    fill_table(table, fields)
    gather_all(table, connect(), vals)
    partial = driver_sums(vals, surface(), driver())
    operator(vals, metric, weights, wide, narrow, back)
    residual(1, drive(), surface(), driver(), back, res)
    local_sums(res, connect(), shared(), partial, local, send, sums, table, sizes)


def last_kernel(ins, outs, scratch, *, sizes, scale):
    recv, shared, current, now0, now1, mass, own, other, recv_before, signal = ins
    out0, out1, grad = outs
    received = received_sums(shared(), recv(), **sizes)
    fields = advance(
        current(), [now0()[...], now1()[...]], mass()[...], own(), other(), received
    )
    for out, field in zip((out0, out1), fields):
        out[...] = field
        out.flush()

    def column(ref):
        row = sum(ref[q, :, 2 * NN :] for q in range(ref.shape[0]))
        ids = [lax.broadcasted_iota(jnp.int32, (8, LANES), axis) for axis in range(2)]
        row = jnp.where(ids[0] == ids[1], jnp.broadcast_to(row, (8, LANES)), 0.0)
        return jnp.sum(row, axis=1, keepdims=True) * scale

    window = signal()
    grad[...] = column(recv()) * window[0:1, :] + column(recv_before()) * window[1:2, :]


class Input:
    def __init__(self, source, buffer, semaphore):
        self.buffer = buffer
        self.copy = pltpu.make_async_copy(source, buffer, semaphore)
        self.waited = False
        self.copy.start()

    def __call__(self):
        if not self.waited:
            self.copy.wait()
            self.waited = True
        return self.buffer


class Output:
    def __init__(self, target, buffer, semaphore):
        self.buffer = buffer
        self.shape = buffer.shape
        self.copy = pltpu.make_async_copy(buffer, target, semaphore)
        self.sent = False

    def __setitem__(self, index, value):
        self.buffer[index] = value

    def flush(self):
        if not self.sent:
            self.copy.start()
            self.sent = True


ANY = pl.BlockSpec(memory_space=pl.ANY)


def call(body, name, arrays, outs, scratch, window=None):
    n_in, n_out = len(arrays), len(outs)
    shapes = [x.shape for x in arrays]
    if window is not None:
        shapes[-1] = (shapes[-1][0], window)

    def kernel(*refs):
        sources, refs = list(refs[:n_in]), refs[n_in:]
        targets, refs = refs[:n_out], refs[n_out:]
        in_buffers, refs = refs[:n_in], refs[n_in:]
        out_buffers, refs = refs[:n_out], refs[n_out:]
        own, (in_sems, out_sems) = refs[:-2], refs[-2:]
        if window is not None:
            start = pl.multiple_of(lax.axis_index(ALL) * window, LANES)
            sources[-1] = sources[-1].at[:, pl.ds(start, window)]
        ins = [Input(s, b, in_sems.at[i]) for i, (s, b) in enumerate(zip(sources, in_buffers))]
        results = [
            Output(t, b, out_sems.at[i]) for i, (t, b) in enumerate(zip(targets, out_buffers))
        ]
        body(ins, results, own)
        for result in results:
            result.flush()
        for result in results:
            result.copy.wait()
        for value in ins:
            value()

    return pl.pallas_call(
        kernel,
        out_shape=[jax.ShapeDtypeStruct(shape, F32) for shape in outs],
        in_specs=[ANY] * n_in,
        out_specs=[ANY] * n_out,
        scratch_shapes=[pltpu.VMEM(shape, x.dtype) for shape, x in zip(shapes, arrays)]
        + [pltpu.VMEM(shape, F32) for shape in outs]
        + [pltpu.VMEM(shape, dtype) for shape, dtype in scratch]
        + [pltpu.SemaphoreType.DMA((n_in,)), pltpu.SemaphoreType.DMA((n_out,))],
        compiler_params=pltpu.CompilerParams(vmem_limit_bytes=64 << 20),
        name=name,
    )(*arrays)


def on_device(
    field_prev,
    field_now,
    adjoint_now,
    adjoint_next,
    inv_mass,
    metric,
    connect,
    surface,
    driver,
    shared,
    filter_taps,
    signal,
):
    wide, narrow, weights = (jnp.asarray(t) for t in element_tables())
    count = connect.shape[0]
    peers = shared.shape[2]
    doms = lax.axis_size("dom")
    devices = lax.axis_size(ALL)
    width = filter_taps.shape[1]
    sizes = dict(doms=doms, peers=peers)
    plane = (LANES, LANES)
    now0, now1, prev0, prev1, mass = (
        x.reshape(plane) for x in (field_now, adjoint_now, field_prev, adjoint_next, inv_mass)
    )
    links = shared.reshape(3, peers, NN)
    driver_row = driver.reshape(1, count)
    if width % LANES == 0:
        window, taps, samples = width, filter_taps, signal
    else:
        window = None
        samples = lax.dynamic_slice_in_dim(signal, lax.axis_index(ALL) * width, width, 1)
        pad = ((0, 0), (0, -width % LANES))
        taps, samples = jnp.pad(filter_taps, pad), jnp.pad(samples, pad)

    def trade(x):
        return lax.all_to_all(x, ALL, 0, 0, tiled=True)

    def swap(x):
        return lax.ppermute(x, "chip", [(0, 1), (1, 0)])

    nodes = (2,) + plane
    elements = ((2, count, NN), F32)
    sums = ((4 * ROWS, COLS), F32)
    table = ((4 * ROWS, COLS), BF)
    packet = (devices, 1, PACKET)
    (terms,) = call(drive_kernel, "drive", [taps, samples], [(devices, 8, LANES)], [], window)
    drive = trade(terms)
    back, partial = call(
        first_kernel,
        "operator0",
        [connect, now0, now1, surface, driver_row, metric, weights, narrow, wide],
        [elements[0], (1, LANES)],
        [elements, table],
    )
    local, send = call(
        functools.partial(second_kernel, sizes=sizes),
        "assemble0",
        [drive, surface, driver_row, back, connect, partial, links],
        [nodes, packet],
        [elements, sums, table],
    )
    other = swap(local)
    recv0 = trade(send)
    current, local, send = call(
        functools.partial(third_kernel, sizes=sizes),
        "step1",
        [recv0, links, now0, now1, prev0, prev1, mass, local, other]
        + [connect, surface, driver_row, metric, weights, narrow, wide, drive],
        [nodes, nodes, packet],
        [elements, elements, elements, sums, table],
    )
    other = swap(local)
    recv1 = trade(send)
    out0, out1, grad = call(
        functools.partial(last_kernel, sizes=sizes, scale=1.0 / math.sqrt(NN * count * devices)),
        "finish",
        [recv1, links, current, now0, now1, mass, local, other, recv0, samples],
        [plane, plane, (8, taps.shape[1])],
        [],
        window,
    )
    grad = grad[:, :width]
    return out0.reshape(1, -1), out1.reshape(1, -1), grad


def solution(mesh):
    region = P(("groups", "dom", "sub"), None)
    element = P(("groups", "dom", "sub", "chip"), None)
    in_specs = (
        region,
        region,
        region,
        region,
        region,
        element,
        element,
        element,
        P(("groups", "dom", "sub", "chip")),
        P(("groups", "dom", "sub"), None, None, None),
        P(None, ALL),
        P(),
    )
    out_specs = (region, region, P("groups", ALL))
    return jax.shard_map(
        on_device, mesh=mesh, in_specs=in_specs, out_specs=out_specs, check_vma=False
    )
```

```python
import functools
import math

import jax
import jax.numpy as jnp
import numpy as np
from jax import lax
from jax.experimental import pallas as pl
from jax.experimental.pallas import tpu as pltpu
from jax.sharding import PartitionSpec as P

NN = 512
LANES = 128
ROWS = 64
COLS = 256
BLOCK = 32
PACKET = 2 * NN + LANES
ALL = ("dom", "sub", "chip")

GLL_POINTS = (
    -1.0,
    -0.8717401485096066,
    -0.5917001814331423,
    -0.2092992179024789,
    0.2092992179024789,
    0.5917001814331423,
    0.8717401485096066,
    1.0,
)
GLL_WEIGHTS = (
    0.03571428571428571,
    0.21070422714350603,
    0.3411226924835044,
    0.4124587946587038,
    0.4124587946587038,
    0.3411226924835044,
    0.21070422714350603,
    0.03571428571428571,
)
BF = jnp.bfloat16
F32 = jnp.float32


def element_tables():
    points = np.array(GLL_POINTS)
    identity = np.eye(8)
    diffs = points[:, None] - points[None, :] + identity
    barycentric = 1.0 / np.prod(diffs, axis=1)
    derivative = barycentric[None, :] / barycentric[:, None] / diffs
    derivative = derivative * (1.0 - identity)
    derivative = derivative - identity * derivative.sum(axis=1)[:, None]
    along_x = np.kron(derivative, np.eye(64)).T
    along_y = np.kron(np.eye(4), np.kron(derivative, identity)).T
    along_z = np.kron(np.eye(32), derivative).T
    quad = np.array(GLL_WEIGHTS)
    cube = np.kron(np.kron(quad, quad), quad)

    def parts(table):
        table = table.astype(np.float32)
        high = table.astype(jnp.bfloat16)
        low = (table - high.astype(np.float32)).astype(jnp.bfloat16)
        return high, low

    wide = list(parts(along_x)) + list(parts(along_x.T))
    narrow = []
    for table in (along_y, along_z, along_y.T, along_z.T):
        narrow += parts(table)
    weights = np.concatenate([cube] * 3).astype(np.float32)[None, :]
    return np.stack(wide), np.stack(narrow), weights


def halves(x):
    high = x.astype(BF)
    return high, (x - high.astype(F32)).astype(BF)


def mm(a, b):
    return jnp.dot(a, b, preferred_element_type=F32)


def times(x, high, low):
    xh, xl = halves(x)
    rows = x.shape[0]
    both = mm(jnp.concatenate([xh, xl], axis=0), high)
    return both[:rows] + both[rows:] + mm(xh, low)


def stack_halves(x):
    return jnp.concatenate([x[:, :256], x[:, 256:]], axis=0)


def unstack_halves(x):
    rows = x.shape[0] // 2
    return jnp.concatenate([x[:rows], x[rows:]], axis=1)


def split_index(index):
    row = (index >> 7) & (ROWS - 1)
    column = (index & (LANES - 1)) | ((index >> 13) << 7)
    return row, column


def column_hot(column):
    ids = lax.broadcasted_iota(jnp.int32, (COLS, NN), 0).astype(BF)
    return jnp.where(ids == column.astype(BF), BF(1), BF(0))


def fill_table(table_ref, fields):
    for k in range(2):
        field = fields[k]
        plane = jnp.concatenate([field[:ROWS], field[ROWS:]], axis=1)
        high, low = halves(plane)
        table_ref[k * ROWS : (k + 1) * ROWS] = high
        table_ref[(2 + k) * ROWS : (3 + k) * ROWS] = low


def look_up(table, index):
    row, column = split_index(index)
    found = mm(table, column_hot(column))
    found = found[: 2 * ROWS] + found[2 * ROWS :]
    mask = lax.broadcasted_iota(jnp.int32, (ROWS, NN), 0) == row
    return [
        jnp.sum(jnp.where(mask, found[k * ROWS : (k + 1) * ROWS], 0.0), axis=0, keepdims=True)
        for k in range(2)
    ]


def spread(indices, values):
    columns = []
    placed = []
    ids = lax.broadcasted_iota(jnp.int32, (ROWS, NN), 0).astype(BF)
    for index, pair in zip(indices, values):
        row, column = split_index(index)
        columns.append(column_hot(column))
        mask = ids == row.astype(BF)
        terms = [halves(v) for v in pair]
        placed.append(
            jnp.concatenate(
                [jnp.where(mask, terms[k][s], BF(0)) for s in range(2) for k in range(2)], axis=0
            )
        )
    left = jnp.concatenate(placed, axis=1) if len(placed) > 1 else placed[0]
    right = jnp.concatenate(columns, axis=1) if len(columns) > 1 else columns[0]
    return lax.dot_general(left, right, (((1,), (1,)), ((), ())), preferred_element_type=F32)


def to_fields(sums):
    sums = sums[: 2 * ROWS] + sums[2 * ROWS :]
    return [
        jnp.concatenate(
            [
                sums[k * ROWS : (k + 1) * ROWS, :LANES],
                sums[k * ROWS : (k + 1) * ROWS, LANES:],
            ],
            axis=0,
        )
        for k in range(2)
    ]


def gather_all(table_ref, connect_ref, vals_ref):
    count = connect_ref.shape[0]
    table = table_ref[...]

    def body(i, carry):
        for u in range(BLOCK):
            e = i * BLOCK + u
            pair = look_up(table, connect_ref[pl.ds(e, 1), :])
            for k in range(2):
                vals_ref[k, pl.ds(e, 1), :] = pair[k]
        return carry

    if count == BLOCK:
        body(0, 0)
    else:
        lax.fori_loop(0, count // BLOCK, body, 0)


def operator(vals_ref, metric, weights, wide, narrow, back_ref):
    count = vals_ref.shape[1]
    vals = jnp.concatenate([vals_ref[0], vals_ref[1]], axis=0)
    stacked = stack_halves(vals)
    metric_ref, weights_ref = metric(), weights()
    total = None
    for i in (1, 2, 0):
        scale = metric_ref[:, i * NN : (i + 1) * NN] * weights_ref[:, i * NN : (i + 1) * NN]
        scale = jnp.concatenate([scale, scale], axis=0)
        if i == 0:
            table = wide()
            part = times(times(vals, table[0], table[1]) * scale, table[2], table[3])
        else:
            table = narrow()
            at = 2 * (i - 1)
            grads = times(stacked, table[at], table[at + 1]) * stack_halves(scale)
            part = unstack_halves(times(grads, table[at + 4], table[at + 5]))
        total = part if total is None else total + part
    back_ref[0] = total[:count]
    back_ref[1] = total[count:]


def driver_hot(driver_ref):
    count = driver_ref.shape[1]
    return (lax.broadcasted_iota(jnp.int32, (8, count), 0) == driver_ref[...]).astype(F32)


def driver_sums(vals_ref, surface_ref, driver_ref):
    products = surface_ref[...] * vals_ref[1]
    products = sum(products[:, i * LANES : (i + 1) * LANES] for i in range(NN // LANES))
    lanes = (((1,), (1,)), ((), ()))
    per_element = lax.dot_general(
        jnp.ones((8, LANES), F32),
        products,
        lanes,
        precision=lax.Precision.HIGHEST,
        preferred_element_type=F32,
    )
    count = driver_ref.shape[1]
    hot = lax.broadcasted_iota(jnp.int32, (LANES, count), 0) == driver_ref[...]
    hot = (hot & (lax.broadcasted_iota(jnp.int32, (LANES, count), 0) < 8)).astype(F32)
    return lax.dot_general(
        per_element, hot, lanes, precision=lax.Precision.HIGHEST, preferred_element_type=F32
    )[:1]


def residual(step, drive_ref, surface_ref, driver_ref, back_ref, res_ref):
    terms = jnp.sum(drive_ref[...], axis=0)
    half = lax.broadcasted_iota(jnp.int32, (8, LANES), 1) >> 6
    terms = jnp.where(half == step, terms, 0.0)
    drive = jnp.broadcast_to(jnp.sum(terms, axis=1, keepdims=True), (8, LANES))
    amplitude = lax.dot_general(
        driver_hot(driver_ref),
        drive,
        (((0,), (0,)), ((), ())),
        precision=lax.Precision.HIGHEST,
        preferred_element_type=F32,
    )
    amplitude = jnp.concatenate([amplitude] * (NN // LANES), axis=1)
    res_ref[0] = amplitude * surface_ref[...] - back_ref[0]
    res_ref[1] = -back_ref[1]


def scatter_all(res_ref, connect_ref, sums_ref):
    count = connect_ref.shape[0]

    def part(i):
        rows = [pl.ds(i * BLOCK + u, 1) for u in range(BLOCK)]
        return spread(
            [connect_ref[r, :] for r in rows],
            [[res_ref[k, r, :] for k in range(2)] for r in rows],
        )

    if count == BLOCK:
        sums_ref[...] = part(0)
        return
    sums_ref[...] = jnp.zeros_like(sums_ref)

    def body(i, carry):
        sums_ref[...] += part(i)
        return carry

    lax.fori_loop(0, count // BLOCK, body, 0)


def fill_send(table_ref, shared_ref, partial, send_ref, *, doms, peers):
    table = table_ref[...]
    empty = jnp.concatenate([jnp.zeros((1, 2 * NN), F32), partial], axis=1)
    for q in range(send_ref.shape[0]):
        send_ref[q] = empty
    slots = [(o, j) for o in (0, 2, 1) for j in range(peers)]
    packets = [
        jnp.concatenate(look_up(table, shared_ref[o, j : j + 1, :]), axis=1) for o, j in slots
    ]
    for (o, j), packet in zip(slots, packets):
        dom = jnp.clip(lax.axis_index("dom") + (o - 1), 0, doms - 1)
        for chip in range(2):
            send_ref[(dom * peers + j) * 2 + chip, :, : 2 * NN] = packet


def received_sums(shared_ref, recv_ref, *, doms, peers):
    indices = []
    values = []
    for o in range(3):
        dom = jnp.clip(lax.axis_index("dom") + (o - 1), 0, doms - 1)
        for j in range(peers):
            start = (dom * peers + j) * 2
            both = recv_ref[start] + recv_ref[start + 1]
            indices.append(shared_ref[o, j : j + 1, :])
            values.append([both[:, k * NN : (k + 1) * NN] for k in range(2)])
    total = None
    for at in range(0, len(indices), 8):
        part = spread(indices[at : at + 8], values[at : at + 8])
        total = part if total is None else total + part
    return to_fields(total)


def advance(current, previous, mass, own, other, received):
    return [
        2.0 * current[k] - previous[k] + mass * (own[k] + other[k] + received[k]) for k in range(2)
    ]


def drive_kernel(ins, outs, scratch):
    taps, signal = (ref() for ref in ins)
    (send,) = outs
    folded = []
    for t in range(2):
        products = taps[...] * signal[t : t + 1, :]
        products = sum(
            products[:, i * LANES : (i + 1) * LANES] for i in range(products.shape[1] // LANES)
        )
        folded.append(products[:, :64] + products[:, 64:])
    terms = jnp.concatenate(folded, axis=1)
    for q in range(send.shape[0]):
        send[q] = terms


def first_kernel(ins, outs, scratch):
    connect, now0, now1, surface, driver, metric, weights, narrow, wide = ins
    back, partial = outs
    vals, table = scratch
    fill_table(table, [now0()[...], now1()[...]])
    gather_all(table, connect(), vals)
    partial[...] = driver_sums(vals, surface(), driver())
    operator(vals, metric, weights, wide, narrow, back)


def local_sums(res, connect, shared, partial, local, send, sums, table, sizes):
    scatter_all(res, connect, sums)
    fields = to_fields(sums[...])
    for k in range(2):
        local[k] = fields[k]
    local.flush()
    fill_table(table, fields)
    fill_send(table, shared, partial, send, **sizes)


def second_kernel(ins, outs, scratch, *, sizes):
    drive, surface, driver, back, connect, partial, shared = ins
    local, send = outs
    res, sums, table = scratch
    residual(0, drive(), surface(), driver(), back(), res)
    local_sums(res, connect(), shared(), partial()[...], local, send, sums, table, sizes)


def third_kernel(ins, outs, scratch, *, sizes):
    recv, shared, now0, now1, prev0, prev1, mass, own, other = ins[:9]
    connect, surface, driver, metric, weights, narrow, wide, drive = ins[9:]
    current, local, send = outs
    vals, back, res, sums, table = scratch
    received = received_sums(shared(), recv(), **sizes)
    fields = advance(
        [now0()[...], now1()[...]],
        [prev0()[...], prev1()[...]],
        mass()[...],
        own(),
        other(),
        received,
    )
    for k in range(2):
        current[k] = fields[k]
    current.flush()
    fill_table(table, fields)
    gather_all(table, connect(), vals)
    partial = driver_sums(vals, surface(), driver())
    operator(vals, metric, weights, wide, narrow, back)
    residual(1, drive(), surface(), driver(), back, res)
    local_sums(res, connect(), shared(), partial, local, send, sums, table, sizes)


def last_kernel(ins, outs, scratch, *, sizes, scale):
    recv, shared, current, now0, now1, mass, own, other, recv_before, signal = ins
    out0, out1, grad = outs
    received = received_sums(shared(), recv(), **sizes)
    fields = advance(
        current(), [now0()[...], now1()[...]], mass()[...], own(), other(), received
    )
    for out, field in zip((out0, out1), fields):
        out[...] = field
        out.flush()

    def column(ref):
        row = sum(ref[q, :, 2 * NN :] for q in range(ref.shape[0]))
        ids = [lax.broadcasted_iota(jnp.int32, (8, LANES), axis) for axis in range(2)]
        row = jnp.where(ids[0] == ids[1], jnp.broadcast_to(row, (8, LANES)), 0.0)
        return jnp.sum(row, axis=1, keepdims=True) * scale

    window = signal()
    grad[...] = column(recv()) * window[0:1, :] + column(recv_before()) * window[1:2, :]


class Input:
    def __init__(self, source, buffer, semaphore):
        self.buffer = buffer
        self.copy = pltpu.make_async_copy(source, buffer, semaphore)
        self.waited = False
        self.copy.start()

    def __call__(self):
        if not self.waited:
            self.copy.wait()
            self.waited = True
        return self.buffer


class Output:
    def __init__(self, target, buffer, semaphore):
        self.buffer = buffer
        self.shape = buffer.shape
        self.copy = None if target is None else pltpu.make_async_copy(buffer, target, semaphore)
        self.sent = False

    def __setitem__(self, index, value):
        self.buffer[index] = value

    def flush(self):
        if self.copy is not None and not self.sent:
            self.copy.start()
            self.sent = True

    def wait(self):
        if self.copy is not None:
            self.copy.wait()


class Held:
    def __init__(self, value):
        self.value = value


ANY = pl.BlockSpec(memory_space=pl.ANY)
VMEM = pl.BlockSpec(memory_space=pltpu.VMEM)


def call(body, name, arrays, outs, scratch, window=None, held=()):
    n_in, n_out = len(arrays), len(outs)
    moved = [i for i, x in enumerate(arrays) if not isinstance(x, Held)]
    sent = [i for i in range(n_out) if i not in held]
    values = [
        pltpu.with_memory_space_constraint(x.value, pltpu.VMEM)
        if isinstance(x, Held)
        else pltpu.with_memory_space_constraint(x, pltpu.HBM)
        for x in arrays
    ]
    shapes = [x.shape for x in values]
    if window is not None:
        shapes[-1] = (shapes[-1][0], window)

    def kernel(*refs):
        sources, refs = list(refs[:n_in]), refs[n_in:]
        targets, refs = refs[:n_out], refs[n_out:]
        in_buffers, refs = refs[: len(moved)], refs[len(moved) :]
        out_buffers, refs = refs[: len(sent)], refs[len(sent) :]
        own, (in_sems, out_sems) = refs[:-2], refs[-2:]
        if window is not None:
            start = pl.multiple_of(lax.axis_index(ALL) * window, LANES)
            sources[-1] = sources[-1].at[:, pl.ds(start, window)]
        ins = [functools.partial(lambda ref: ref, ref) for ref in sources]
        for at, i in enumerate(moved):
            ins[i] = Input(sources[i], in_buffers[at], in_sems.at[at])
        results = [Output(None, ref, None) for ref in targets]
        for at, i in enumerate(sent):
            results[i] = Output(targets[i], out_buffers[at], out_sems.at[at])
        body(ins, results, own)
        for result in results:
            result.flush()
        for result in results:
            result.wait()
        for value in ins:
            value()

    results = pl.pallas_call(
        kernel,
        out_shape=[
            pltpu.VMEM(shape, F32) if i in held else jax.ShapeDtypeStruct(shape, F32)
            for i, shape in enumerate(outs)
        ],
        in_specs=[VMEM if isinstance(x, Held) else ANY for x in arrays],
        out_specs=[VMEM if i in held else ANY for i in range(n_out)],
        scratch_shapes=[pltpu.VMEM(shapes[i], values[i].dtype) for i in moved]
        + [pltpu.VMEM(outs[i], F32) for i in sent]
        + [pltpu.VMEM(shape, dtype) for shape, dtype in scratch]
        + [
            pltpu.SemaphoreType.DMA((max(len(moved), 1),)),
            pltpu.SemaphoreType.DMA((max(len(sent), 1),)),
        ],
        compiler_params=pltpu.CompilerParams(vmem_limit_bytes=40 << 20),
        name=name,
    )(*values)
    return [Held(x) if i in held else x for i, x in enumerate(results)]


def on_device(
    field_prev,
    field_now,
    adjoint_now,
    adjoint_next,
    inv_mass,
    metric,
    connect,
    surface,
    driver,
    shared,
    filter_taps,
    signal,
):
    wide, narrow, weights = (jnp.asarray(t) for t in element_tables())
    count = connect.shape[0]
    peers = shared.shape[2]
    doms = lax.axis_size("dom")
    devices = lax.axis_size(ALL)
    width = filter_taps.shape[1]
    sizes = dict(doms=doms, peers=peers)
    plane = (LANES, LANES)
    now0, now1, prev0, prev1, mass = (
        x.reshape(plane) for x in (field_now, adjoint_now, field_prev, adjoint_next, inv_mass)
    )
    links = shared.reshape(3, peers, NN)
    driver_row = driver.reshape(1, count)
    if width % LANES == 0:
        window, taps, samples = width, filter_taps, signal
    else:
        window = None
        samples = lax.dynamic_slice_in_dim(signal, lax.axis_index(ALL) * width, width, 1)
        pad = ((0, 0), (0, -width % LANES))
        taps, samples = jnp.pad(filter_taps, pad), jnp.pad(samples, pad)

    def trade(x):
        return Held(lax.all_to_all(x.value, ALL, 0, 0, tiled=True))

    def swap(x):
        return Held(lax.ppermute(x.value, "chip", [(0, 1), (1, 0)]))

    nodes = (2,) + plane
    elements = ((2, count, NN), F32)
    sums = ((4 * ROWS, COLS), F32)
    table = ((4 * ROWS, COLS), BF)
    packet = (devices, 1, PACKET)
    (terms,) = call(drive_kernel, "drive", [taps, samples], [(devices, 8, LANES)], [], window, (0,))
    drive = trade(terms)
    back, partial = call(
        first_kernel,
        "operator0",
        [connect, now0, now1, surface, driver_row, metric, weights, narrow, wide],
        [elements[0], (1, LANES)],
        [elements, table],
        held=(0, 1),
    )
    local, send = call(
        functools.partial(second_kernel, sizes=sizes),
        "assemble0",
        [drive, surface, driver_row, back, connect, partial, links],
        [nodes, packet],
        [elements, sums, table],
        held=(0, 1),
    )
    other = swap(local)
    recv0 = trade(send)
    current, local, send = call(
        functools.partial(third_kernel, sizes=sizes),
        "step1",
        [recv0, links, now0, now1, prev0, prev1, mass, local, other]
        + [connect, surface, driver_row, metric, weights, narrow, wide, drive],
        [nodes, nodes, packet],
        [elements, elements, elements, sums, table],
        held=(0, 1, 2),
    )
    other = swap(local)
    recv1 = trade(send)
    out0, out1, grad = call(
        functools.partial(last_kernel, sizes=sizes, scale=1.0 / math.sqrt(NN * count * devices)),
        "finish",
        [recv1, links, current, now0, now1, mass, local, other, recv0, samples],
        [plane, plane, (8, taps.shape[1])],
        [],
        window,
    )
    grad = grad[:, :width]
    return out0.reshape(1, -1), out1.reshape(1, -1), grad


def solution(mesh):
    region = P(("groups", "dom", "sub"), None)
    element = P(("groups", "dom", "sub", "chip"), None)
    in_specs = (
        region,
        region,
        region,
        region,
        region,
        element,
        element,
        element,
        P(("groups", "dom", "sub", "chip")),
        P(("groups", "dom", "sub"), None, None, None),
        P(None, ALL),
        P(),
    )
    out_specs = (region, region, P("groups", ALL))
    return jax.shard_map(
        on_device, mesh=mesh, in_specs=in_specs, out_specs=out_specs, check_vma=False
    )
```

```python
import functools
import math

import jax
import jax.numpy as jnp
import numpy as np
from jax import lax
from jax.experimental import pallas as pl
from jax.experimental.pallas import tpu as pltpu
from jax.sharding import PartitionSpec as P

NN = 512
LANES = 128
ROWS = 64
COLS = 256
BLOCK = 32
PACKET = 2 * NN + LANES
ALL = ("dom", "sub", "chip")

GLL_POINTS = (
    -1.0,
    -0.8717401485096066,
    -0.5917001814331423,
    -0.2092992179024789,
    0.2092992179024789,
    0.5917001814331423,
    0.8717401485096066,
    1.0,
)
GLL_WEIGHTS = (
    0.03571428571428571,
    0.21070422714350603,
    0.3411226924835044,
    0.4124587946587038,
    0.4124587946587038,
    0.3411226924835044,
    0.21070422714350603,
    0.03571428571428571,
)
BF = jnp.bfloat16
F32 = jnp.float32


def element_tables():
    points = np.array(GLL_POINTS)
    identity = np.eye(8)
    diffs = points[:, None] - points[None, :] + identity
    barycentric = 1.0 / np.prod(diffs, axis=1)
    derivative = barycentric[None, :] / barycentric[:, None] / diffs
    derivative = derivative * (1.0 - identity)
    derivative = derivative - identity * derivative.sum(axis=1)[:, None]
    along_x = np.kron(derivative, np.eye(64)).T
    along_y = np.kron(np.eye(4), np.kron(derivative, identity)).T
    along_z = np.kron(np.eye(32), derivative).T
    quad = np.array(GLL_WEIGHTS)
    cube = np.kron(np.kron(quad, quad), quad)

    def parts(table):
        table = table.astype(np.float32)
        high = table.astype(jnp.bfloat16)
        low = (table - high.astype(np.float32)).astype(jnp.bfloat16)
        return high, low

    wide = list(parts(along_x)) + list(parts(along_x.T))
    narrow = []
    for table in (along_y, along_z, along_y.T, along_z.T):
        narrow += parts(table)
    weights = np.concatenate([cube] * 3).astype(np.float32)[None, :]
    return np.stack(wide), np.stack(narrow), weights


def halves(x):
    high = x.astype(BF)
    return high, (x - high.astype(F32)).astype(BF)


def mm(a, b):
    return jnp.dot(a, b, preferred_element_type=F32)


def times(x, high, low):
    xh, xl = halves(x)
    rows = x.shape[0]
    both = mm(jnp.concatenate([xh, xl], axis=0), high)
    return both[:rows] + both[rows:] + mm(xh, low)


def stack_halves(x):
    return jnp.concatenate([x[:, :256], x[:, 256:]], axis=0)


def unstack_halves(x):
    rows = x.shape[0] // 2
    return jnp.concatenate([x[:rows], x[rows:]], axis=1)


def split_index(index):
    row = (index >> 7) & (ROWS - 1)
    column = (index & (LANES - 1)) | ((index >> 13) << 7)
    return row, column


def column_hot(column):
    ids = lax.broadcasted_iota(jnp.int32, (COLS, NN), 0).astype(BF)
    return jnp.where(ids == column.astype(BF), BF(1), BF(0))


def fill_table(table_ref, fields):
    for k in range(2):
        field = fields[k]
        plane = jnp.concatenate([field[:ROWS], field[ROWS:]], axis=1)
        high, low = halves(plane)
        table_ref[k * ROWS : (k + 1) * ROWS] = high
        table_ref[(2 + k) * ROWS : (3 + k) * ROWS] = low


def look_up(table, index):
    row, column = split_index(index)
    found = mm(table, column_hot(column))
    found = found[: 2 * ROWS] + found[2 * ROWS :]
    mask = lax.broadcasted_iota(jnp.int32, (ROWS, NN), 0) == row
    return [
        jnp.sum(jnp.where(mask, found[k * ROWS : (k + 1) * ROWS], 0.0), axis=0, keepdims=True)
        for k in range(2)
    ]


def spread(indices, values):
    columns = []
    placed = []
    ids = lax.broadcasted_iota(jnp.int32, (ROWS, NN), 0).astype(BF)
    for index, pair in zip(indices, values):
        row, column = split_index(index)
        columns.append(column_hot(column))
        mask = ids == row.astype(BF)
        terms = [halves(v) for v in pair]
        placed.append(
            jnp.concatenate(
                [jnp.where(mask, terms[k][s], BF(0)) for s in range(2) for k in range(2)], axis=0
            )
        )
    left = jnp.concatenate(placed, axis=1) if len(placed) > 1 else placed[0]
    right = jnp.concatenate(columns, axis=1) if len(columns) > 1 else columns[0]
    return lax.dot_general(left, right, (((1,), (1,)), ((), ())), preferred_element_type=F32)


def to_fields(sums):
    sums = sums[: 2 * ROWS] + sums[2 * ROWS :]
    return [
        jnp.concatenate(
            [
                sums[k * ROWS : (k + 1) * ROWS, :LANES],
                sums[k * ROWS : (k + 1) * ROWS, LANES:],
            ],
            axis=0,
        )
        for k in range(2)
    ]


def gather_all(table_ref, connect_ref, vals_ref):
    count = connect_ref.shape[0]
    table = table_ref[...]

    def body(i, carry):
        for u in range(BLOCK):
            e = i * BLOCK + u
            pair = look_up(table, connect_ref[pl.ds(e, 1), :])
            for k in range(2):
                vals_ref[k, pl.ds(e, 1), :] = pair[k]
        return carry

    if count == BLOCK:
        body(0, 0)
    else:
        lax.fori_loop(0, count // BLOCK, body, 0)


def operator(vals_ref, metric, weights, wide, narrow, back_ref):
    count = vals_ref.shape[1]
    vals = jnp.concatenate([vals_ref[0], vals_ref[1]], axis=0)
    stacked = stack_halves(vals)
    metric_ref, weights_ref = metric(), weights()
    total = None
    for i in (1, 2, 0):
        scale = metric_ref[:, i * NN : (i + 1) * NN] * weights_ref[:, i * NN : (i + 1) * NN]
        scale = jnp.concatenate([scale, scale], axis=0)
        if i == 0:
            table = wide()
            part = times(times(vals, table[0], table[1]) * scale, table[2], table[3])
        else:
            table = narrow()
            at = 2 * (i - 1)
            grads = times(stacked, table[at], table[at + 1]) * stack_halves(scale)
            part = unstack_halves(times(grads, table[at + 4], table[at + 5]))
        total = part if total is None else total + part
    back_ref[0] = total[:count]
    back_ref[1] = total[count:]


def driver_hot(driver_ref):
    count = driver_ref.shape[1]
    return (lax.broadcasted_iota(jnp.int32, (8, count), 0) == driver_ref[...]).astype(F32)


def driver_sums(vals_ref, surface_ref, driver_ref):
    products = surface_ref[...] * vals_ref[1]
    products = sum(products[:, i * LANES : (i + 1) * LANES] for i in range(NN // LANES))
    lanes = (((1,), (1,)), ((), ()))
    per_element = lax.dot_general(
        jnp.ones((8, LANES), F32),
        products,
        lanes,
        precision=lax.Precision.HIGHEST,
        preferred_element_type=F32,
    )
    count = driver_ref.shape[1]
    hot = lax.broadcasted_iota(jnp.int32, (LANES, count), 0) == driver_ref[...]
    hot = (hot & (lax.broadcasted_iota(jnp.int32, (LANES, count), 0) < 8)).astype(F32)
    return lax.dot_general(
        per_element, hot, lanes, precision=lax.Precision.HIGHEST, preferred_element_type=F32
    )[:1]


def residual(step, drive_ref, surface_ref, driver_ref, back_ref, res_ref):
    terms = jnp.sum(drive_ref[...], axis=0)
    half = lax.broadcasted_iota(jnp.int32, (8, LANES), 1) >> 6
    terms = jnp.where(half == step, terms, 0.0)
    drive = jnp.broadcast_to(jnp.sum(terms, axis=1, keepdims=True), (8, LANES))
    amplitude = lax.dot_general(
        driver_hot(driver_ref),
        drive,
        (((0,), (0,)), ((), ())),
        precision=lax.Precision.HIGHEST,
        preferred_element_type=F32,
    )
    amplitude = jnp.concatenate([amplitude] * (NN // LANES), axis=1)
    res_ref[0] = amplitude * surface_ref[...] - back_ref[0]
    res_ref[1] = -back_ref[1]


def scatter_all(res_ref, connect_ref, sums_ref):
    count = connect_ref.shape[0]

    def part(i):
        rows = [pl.ds(i * BLOCK + u, 1) for u in range(BLOCK)]
        return spread(
            [connect_ref[r, :] for r in rows],
            [[res_ref[k, r, :] for k in range(2)] for r in rows],
        )

    if count == BLOCK:
        sums_ref[...] = part(0)
        return
    sums_ref[...] = jnp.zeros_like(sums_ref)

    def body(i, carry):
        sums_ref[...] += part(i)
        return carry

    lax.fori_loop(0, count // BLOCK, body, 0)


def fill_send(table_ref, shared_ref, partial, send_ref, *, doms, peers):
    table = table_ref[...]
    empty = jnp.concatenate([jnp.zeros((1, 2 * NN), F32), partial], axis=1)
    for q in range(send_ref.shape[0]):
        send_ref[q] = empty
    slots = [(o, j) for o in (0, 2, 1) for j in range(peers)]
    packets = [
        jnp.concatenate(look_up(table, shared_ref[o, j : j + 1, :]), axis=1) for o, j in slots
    ]
    for (o, j), packet in zip(slots, packets):
        dom = jnp.clip(lax.axis_index("dom") + (o - 1), 0, doms - 1)
        for chip in range(2):
            send_ref[(dom * peers + j) * 2 + chip, :, : 2 * NN] = packet


def received_sums(shared_ref, recv_ref, *, doms, peers):
    indices = []
    values = []
    for o in range(3):
        dom = jnp.clip(lax.axis_index("dom") + (o - 1), 0, doms - 1)
        for j in range(peers):
            start = (dom * peers + j) * 2
            both = recv_ref[start] + recv_ref[start + 1]
            indices.append(shared_ref[o, j : j + 1, :])
            values.append([both[:, k * NN : (k + 1) * NN] for k in range(2)])
    total = None
    for at in range(0, len(indices), 8):
        part = spread(indices[at : at + 8], values[at : at + 8])
        total = part if total is None else total + part
    return to_fields(total)


def advance(base, mass, received):
    return [base[k] + mass * received[k] for k in range(2)]


def fill_base(base, current, previous, mass, own, other):
    for k in range(2):
        base[k] = 2.0 * current[k] - previous[k] + mass * (own[k] + other[k])


def base_kernel(ins, outs, scratch):
    own, other, mass, now0, now1, prev0, prev1 = (ref() for ref in ins[:7])
    current, previous = [now0[...], now1[...]], [prev0[...], prev1[...]]
    fill_base(outs[0], current, previous, mass[...], own, other)


def last_base_kernel(ins, outs, scratch):
    own, other, mass, current, now0, now1 = (ref() for ref in ins[:6])
    fill_base(outs[0], current, [now0[...], now1[...]], mass[...], own, other)


def drive_kernel(ins, outs, scratch):
    taps, signal = ins[0](), ins[-1]()
    (send,) = outs
    folded = []
    for t in range(2):
        products = taps[...] * signal[t : t + 1, :]
        products = sum(
            products[:, i * LANES : (i + 1) * LANES] for i in range(products.shape[1] // LANES)
        )
        folded.append(products[:, :64] + products[:, 64:])
    terms = jnp.concatenate(folded, axis=1)
    for q in range(send.shape[0]):
        send[q] = terms


def first_kernel(ins, outs, scratch):
    connect, now0, now1, surface, driver, metric, weights, narrow, wide = ins[:9]
    back, partial = outs
    vals, table = scratch
    fill_table(table, [now0()[...], now1()[...]])
    gather_all(table, connect(), vals)
    partial[...] = driver_sums(vals, surface(), driver())
    operator(vals, metric, weights, wide, narrow, back)


def local_sums(res, connect, shared, partial, local, send, sums, table, sizes):
    scatter_all(res, connect, sums)
    fields = to_fields(sums[...])
    for k in range(2):
        local[k] = fields[k]
    local.flush()
    fill_table(table, fields)
    fill_send(table, shared, partial, send, **sizes)


def second_kernel(ins, outs, scratch, *, sizes):
    drive, surface, driver, back, connect, partial, shared = ins
    local, send = outs
    res, sums, table = scratch
    residual(0, drive(), surface(), driver(), back(), res)
    local_sums(res, connect(), shared(), partial()[...], local, send, sums, table, sizes)


def third_kernel(ins, outs, scratch, *, sizes):
    recv, base, mass, shared, connect, surface, driver, metric, weights, narrow, wide, drive = ins
    current, local, send = outs
    vals, back, res, sums, table = scratch
    received = received_sums(shared(), recv(), **sizes)
    fields = advance(base(), mass()[...], received)
    for k in range(2):
        current[k] = fields[k]
    current.flush()
    fill_table(table, fields)
    gather_all(table, connect(), vals)
    partial = driver_sums(vals, surface(), driver())
    operator(vals, metric, weights, wide, narrow, back)
    residual(1, drive(), surface(), driver(), back, res)
    local_sums(res, connect(), shared(), partial, local, send, sums, table, sizes)


def last_kernel(ins, outs, scratch, *, sizes, scale):
    recv, base, mass, shared, recv_before, signal = ins
    out0, out1, grad = outs
    received = received_sums(shared(), recv(), **sizes)
    fields = advance(base(), mass()[...], received)
    for out, field in zip((out0, out1), fields):
        out[...] = field
        out.flush()

    def column(ref):
        row = sum(ref[q, :, 2 * NN :] for q in range(ref.shape[0]))
        ids = [lax.broadcasted_iota(jnp.int32, (8, LANES), axis) for axis in range(2)]
        row = jnp.where(ids[0] == ids[1], jnp.broadcast_to(row, (8, LANES)), 0.0)
        return jnp.sum(row, axis=1, keepdims=True) * scale

    window = signal()
    grad[...] = column(recv()) * window[0:1, :] + column(recv_before()) * window[1:2, :]


class Input:
    def __init__(self, source, buffer, semaphore):
        self.buffer = buffer
        self.copy = pltpu.make_async_copy(source, buffer, semaphore)
        self.waited = False
        self.copy.start()

    def __call__(self):
        if not self.waited:
            self.copy.wait()
            self.waited = True
        return self.buffer


class Output:
    def __init__(self, target, buffer, semaphore):
        self.buffer = buffer
        self.shape = buffer.shape
        self.copy = None if target is None else pltpu.make_async_copy(buffer, target, semaphore)
        self.sent = False

    def __setitem__(self, index, value):
        self.buffer[index] = value

    def flush(self):
        if self.copy is not None and not self.sent:
            self.copy.start()
            self.sent = True

    def wait(self):
        if self.copy is not None:
            self.copy.wait()


class Held:
    def __init__(self, value):
        self.value = value


ANY = pl.BlockSpec(memory_space=pl.ANY)
VMEM = pl.BlockSpec(memory_space=pltpu.VMEM)


def call(body, name, arrays, outs, scratch, window=None, held=(), keep=()):
    n_in, n_out = len(arrays), len(outs)
    fetched = [i for i, x in enumerate(arrays) if not isinstance(x, Held)]
    moved = [i for i in fetched if i not in keep]
    sent = [i for i in range(n_out) if i not in held]
    values = [
        pltpu.with_memory_space_constraint(x.value, pltpu.VMEM)
        if isinstance(x, Held)
        else pltpu.with_memory_space_constraint(x, pltpu.HBM)
        for x in arrays
    ]
    shapes = [x.shape for x in values]
    if window is not None:
        shapes[-1] = (shapes[-1][0], window)

    def kernel(*refs):
        sources, refs = list(refs[:n_in]), refs[n_in:]
        targets, refs = refs[:n_out], refs[n_out:]
        kept, refs = refs[: len(keep)], refs[len(keep) :]
        in_buffers, refs = refs[: len(moved)], refs[len(moved) :]
        out_buffers, refs = refs[: len(sent)], refs[len(sent) :]
        own, (in_sems, out_sems) = refs[:-2], refs[-2:]
        if window is not None:
            start = pl.multiple_of(lax.axis_index(ALL) * window, LANES)
            sources[-1] = sources[-1].at[:, pl.ds(start, window)]
        ins = [functools.partial(lambda ref: ref, ref) for ref in sources]
        buffers = dict(zip(moved, in_buffers)) | dict(zip(keep, kept))
        for at, i in enumerate(fetched):
            ins[i] = Input(sources[i], buffers[i], in_sems.at[at])
        results = [Output(None, ref, None) for ref in targets]
        for at, i in enumerate(sent):
            results[i] = Output(targets[i], out_buffers[at], out_sems.at[at])
        body(ins, results, own)
        for result in results:
            result.flush()
        for result in results:
            result.wait()
        for value in ins:
            value()

    results = pl.pallas_call(
        kernel,
        out_shape=[
            pltpu.VMEM(shape, F32) if i in held else jax.ShapeDtypeStruct(shape, F32)
            for i, shape in enumerate(outs)
        ]
        + [pltpu.VMEM(shapes[i], values[i].dtype) for i in keep],
        in_specs=[VMEM if isinstance(x, Held) else ANY for x in arrays],
        out_specs=[VMEM if i in held else ANY for i in range(n_out)] + [VMEM] * len(keep),
        scratch_shapes=[pltpu.VMEM(shapes[i], values[i].dtype) for i in moved]
        + [pltpu.VMEM(outs[i], F32) for i in sent]
        + [pltpu.VMEM(shape, dtype) for shape, dtype in scratch]
        + [
            pltpu.SemaphoreType.DMA((max(len(fetched), 1),)),
            pltpu.SemaphoreType.DMA((max(len(sent), 1),)),
        ],
        compiler_params=pltpu.CompilerParams(vmem_limit_bytes=40 << 20),
        name=name,
    )(*values)
    return [Held(x) if i in held or i >= n_out else x for i, x in enumerate(results)]


def on_device(
    field_prev,
    field_now,
    adjoint_now,
    adjoint_next,
    inv_mass,
    metric,
    connect,
    surface,
    driver,
    shared,
    filter_taps,
    signal,
):
    wide, narrow, weights = (jnp.asarray(t) for t in element_tables())
    count = connect.shape[0]
    peers = shared.shape[2]
    doms = lax.axis_size("dom")
    devices = lax.axis_size(ALL)
    width = filter_taps.shape[1]
    sizes = dict(doms=doms, peers=peers)
    plane = (LANES, LANES)
    now0, now1, prev0, prev1, mass = (
        x.reshape(plane) for x in (field_now, adjoint_now, field_prev, adjoint_next, inv_mass)
    )
    links = shared.reshape(3, peers, NN)
    driver_row = driver.reshape(1, count)
    if width % LANES == 0:
        window, taps, samples = width, filter_taps, signal
    else:
        window = None
        samples = lax.dynamic_slice_in_dim(signal, lax.axis_index(ALL) * width, width, 1)
        pad = ((0, 0), (0, -width % LANES))
        taps, samples = jnp.pad(filter_taps, pad), jnp.pad(samples, pad)

    def trade(x):
        return Held(lax.all_to_all(x.value, ALL, 0, 0, tiled=True))

    def swap(x):
        return Held(lax.ppermute(x.value, "chip", [(0, 1), (1, 0)]))

    nodes = (2,) + plane
    elements = ((2, count, NN), F32)
    sums = ((4 * ROWS, COLS), F32)
    table = ((4 * ROWS, COLS), BF)
    packet = (devices, 1, PACKET)
    terms, connect0, now0_held, now1_held = call(
        drive_kernel,
        "drive",
        [taps, connect, now0, now1, samples],
        [(devices, 8, LANES)],
        [],
        window,
        held=(0,),
        keep=(1, 2, 3),
    )
    drive = trade(terms)
    back, partial, surface0, driver0, links0 = call(
        first_kernel,
        "operator0",
        [connect0, now0_held, now1_held, surface, driver_row, metric, weights, narrow, wide, links],
        [elements[0], (1, LANES)],
        [elements, table],
        held=(0, 1),
        keep=(3, 4, 9),
    )
    local, send = call(
        functools.partial(second_kernel, sizes=sizes),
        "assemble0",
        [drive, surface0, driver0, back, connect0, partial, links0],
        [nodes, packet],
        [elements, sums, table],
        held=(0, 1),
    )
    other = swap(local)
    recv0 = trade(send)
    base, *rest = call(
        base_kernel,
        "base0",
        [local, other, mass, now0, now1, prev0, prev1, links, connect],
        [nodes],
        [],
        held=(0,),
        keep=(2, 7, 8),
    )
    current, local, send = call(
        functools.partial(third_kernel, sizes=sizes),
        "step1",
        [recv0, base, *rest, surface, driver_row, metric, weights, narrow, wide, drive],
        [nodes, nodes, packet],
        [elements, elements, elements, sums, table],
        held=(0, 1, 2),
    )
    other = swap(local)
    recv1 = trade(send)
    base, mass1, links1, samples1 = call(
        last_base_kernel,
        "base1",
        [local, other, mass, current, now0, now1, links, samples],
        [nodes],
        [],
        window,
        held=(0,),
        keep=(2, 6, 7),
    )
    out0, out1, grad = call(
        functools.partial(last_kernel, sizes=sizes, scale=1.0 / math.sqrt(NN * count * devices)),
        "finish",
        [recv1, base, mass1, links1, recv0, samples1],
        [plane, plane, (8, taps.shape[1])],
        [],
    )
    grad = grad[:, :width]
    return out0.reshape(1, -1), out1.reshape(1, -1), grad


def solution(mesh):
    region = P(("groups", "dom", "sub"), None)
    element = P(("groups", "dom", "sub", "chip"), None)
    in_specs = (
        region,
        region,
        region,
        region,
        region,
        element,
        element,
        element,
        P(("groups", "dom", "sub", "chip")),
        P(("groups", "dom", "sub"), None, None, None),
        P(None, ALL),
        P(),
    )
    out_specs = (region, region, P("groups", ALL))
    return jax.shard_map(
        on_device, mesh=mesh, in_specs=in_specs, out_specs=out_specs, check_vma=False
    )
```

```python
import functools
import math

import jax
import jax.numpy as jnp
import numpy as np
from jax import lax
from jax.experimental import pallas as pl
from jax.experimental.pallas import tpu as pltpu
from jax.sharding import PartitionSpec as P

NN = 512
LANES = 128
ROWS = 64
COLS = 256
BLOCK = 32
PACKET = 2 * NN + LANES
ALL = ("dom", "sub", "chip")

GLL_POINTS = (
    -1.0,
    -0.8717401485096066,
    -0.5917001814331423,
    -0.2092992179024789,
    0.2092992179024789,
    0.5917001814331423,
    0.8717401485096066,
    1.0,
)
GLL_WEIGHTS = (
    0.03571428571428571,
    0.21070422714350603,
    0.3411226924835044,
    0.4124587946587038,
    0.4124587946587038,
    0.3411226924835044,
    0.21070422714350603,
    0.03571428571428571,
)
BF = jnp.bfloat16
F32 = jnp.float32


def element_tables():
    points = np.array(GLL_POINTS)
    identity = np.eye(8)
    diffs = points[:, None] - points[None, :] + identity
    barycentric = 1.0 / np.prod(diffs, axis=1)
    derivative = barycentric[None, :] / barycentric[:, None] / diffs
    derivative = derivative * (1.0 - identity)
    derivative = derivative - identity * derivative.sum(axis=1)[:, None]
    along_x = np.kron(derivative, np.eye(64)).T
    along_y = np.kron(np.eye(4), np.kron(derivative, identity)).T
    along_z = np.kron(np.eye(32), derivative).T
    quad = np.array(GLL_WEIGHTS)
    cube = np.kron(np.kron(quad, quad), quad)

    def parts(table):
        table = table.astype(np.float32)
        high = table.astype(jnp.bfloat16)
        low = (table - high.astype(np.float32)).astype(jnp.bfloat16)
        return high, low

    wide = list(parts(along_x)) + list(parts(along_x.T))
    forward = parts(np.concatenate([along_y, along_z], axis=1))
    backward = parts(np.concatenate([along_y.T, along_z.T], axis=0))
    weights = np.concatenate([cube] * 3).astype(np.float32)[None, :]
    return np.stack(wide), np.stack(forward), np.stack(backward), weights


def halves(x):
    high = x.astype(BF)
    return high, (x - high.astype(F32)).astype(BF)


def mm(a, b):
    return jnp.dot(a, b, preferred_element_type=F32)


def times(x, high, low):
    xh, xl = halves(x)
    rows = x.shape[0]
    both = mm(jnp.concatenate([xh, xl], axis=0), high)
    return both[:rows] + both[rows:] + mm(xh, low)


def stack_halves(x):
    return jnp.concatenate([x[:, :256], x[:, 256:]], axis=0)


def unstack_halves(x):
    rows = x.shape[0] // 2
    return jnp.concatenate([x[:rows], x[rows:]], axis=1)


def split_index(index):
    row = (index >> 7) & (ROWS - 1)
    column = (index & (LANES - 1)) | ((index >> 13) << 7)
    return row, column


def column_hot(column):
    ids = lax.broadcasted_iota(jnp.int32, (COLS, NN), 0).astype(BF)
    return jnp.where(ids == column.astype(BF), BF(1), BF(0))


def fill_table(table_ref, fields):
    for k in range(2):
        field = fields[k]
        plane = jnp.concatenate([field[:ROWS], field[ROWS:]], axis=1)
        high, low = halves(plane)
        table_ref[k * ROWS : (k + 1) * ROWS] = high
        table_ref[(2 + k) * ROWS : (3 + k) * ROWS] = low


def look_up(table, index):
    row, column = split_index(index)
    found = mm(table, column_hot(column))
    found = found[: 2 * ROWS] + found[2 * ROWS :]
    mask = lax.broadcasted_iota(jnp.int32, (ROWS, NN), 0) == row
    return [
        jnp.sum(jnp.where(mask, found[k * ROWS : (k + 1) * ROWS], 0.0), axis=0, keepdims=True)
        for k in range(2)
    ]


def spread(indices, values):
    columns = []
    placed = []
    ids = lax.broadcasted_iota(jnp.int32, (ROWS, NN), 0).astype(BF)
    for index, pair in zip(indices, values):
        row, column = split_index(index)
        columns.append(column_hot(column))
        mask = ids == row.astype(BF)
        terms = [halves(v) for v in pair]
        placed.append(
            jnp.concatenate(
                [jnp.where(mask, terms[k][s], BF(0)) for s in range(2) for k in range(2)], axis=0
            )
        )
    left = jnp.concatenate(placed, axis=1) if len(placed) > 1 else placed[0]
    right = jnp.concatenate(columns, axis=1) if len(columns) > 1 else columns[0]
    return lax.dot_general(left, right, (((1,), (1,)), ((), ())), preferred_element_type=F32)


def to_fields(sums):
    sums = sums[: 2 * ROWS] + sums[2 * ROWS :]
    return [
        jnp.concatenate(
            [
                sums[k * ROWS : (k + 1) * ROWS, :LANES],
                sums[k * ROWS : (k + 1) * ROWS, LANES:],
            ],
            axis=0,
        )
        for k in range(2)
    ]


def gather_all(table_ref, connect_ref, vals_ref):
    count = connect_ref.shape[0]
    table = table_ref[...]

    def body(i, carry):
        for u in range(BLOCK):
            e = i * BLOCK + u
            pair = look_up(table, connect_ref[pl.ds(e, 1), :])
            for k in range(2):
                vals_ref[k, pl.ds(e, 1), :] = pair[k]
        return carry

    if count == BLOCK:
        body(0, 0)
    else:
        lax.fori_loop(0, count // BLOCK, body, 0)


def operator(vals_ref, metric, weights, narrow, narrow_back, wide, back_ref):
    count = vals_ref.shape[1]
    vals = jnp.concatenate([vals_ref[0], vals_ref[1]], axis=0)
    scale = metric()[...] * weights()[...]
    scale = jnp.concatenate([scale, scale], axis=0)
    along = [scale[:, i * NN : (i + 1) * NN] for i in range(3)]
    table = narrow()
    grads = times(stack_halves(vals), table[0], table[1])
    grads = grads * jnp.concatenate([stack_halves(x) for x in along[1:]], axis=1)
    table = narrow_back()
    total = unstack_halves(times(grads, table[0], table[1]))
    table = wide()
    total += times(times(vals, table[0], table[1]) * along[0], table[2], table[3])
    back_ref[0] = total[:count]
    back_ref[1] = total[count:]


def driver_hot(driver_ref):
    count = driver_ref.shape[1]
    ids = lax.broadcasted_iota(jnp.int32, (LANES, count), 0)
    return ((ids == driver_ref[...]) & (ids < 8)).astype(F32).T


def driver_sums(vals_ref, surface_ref, hot):
    products = surface_ref[...] * vals_ref[1]
    products = sum(products[:, i * LANES : (i + 1) * LANES] for i in range(NN // LANES))
    return jnp.sum(hot * jnp.sum(products, axis=1, keepdims=True), axis=0, keepdims=True)


def amplitudes(step, drive_ref, hot):
    terms = jnp.sum(drive_ref[...], axis=0)
    half = lax.broadcasted_iota(jnp.int32, (8, LANES), 1) >> 6
    drive = jnp.sum(jnp.where(half == step, terms, 0.0), axis=1, keepdims=True)
    ids = [lax.broadcasted_iota(jnp.int32, (8, LANES), axis) for axis in range(2)]
    row = jnp.sum(jnp.where(ids[0] == ids[1], drive, 0.0), axis=0, keepdims=True)
    return jnp.sum(hot * row, axis=1, keepdims=True)


def residual(amplitude, surface_ref, back_ref, res_ref):
    res_ref[0] = amplitude * surface_ref[...] - back_ref[0]
    res_ref[1] = -back_ref[1]


def scatter_all(res_ref, connect_ref, sums_ref):
    count = connect_ref.shape[0]

    def part(i):
        rows = [pl.ds(i * BLOCK + u, 1) for u in range(BLOCK)]
        return spread(
            [connect_ref[r, :] for r in rows],
            [[res_ref[k, r, :] for k in range(2)] for r in rows],
        )

    if count == BLOCK:
        sums_ref[...] = part(0)
        return
    sums_ref[...] = jnp.zeros_like(sums_ref)

    def body(i, carry):
        sums_ref[...] += part(i)
        return carry

    lax.fori_loop(0, count // BLOCK, body, 0)


def fill_send(table_ref, shared_ref, partial, send_ref, *, doms, peers):
    table = table_ref[...]
    empty = jnp.concatenate([jnp.zeros((1, 2 * NN), F32), partial], axis=1)
    for q in range(send_ref.shape[0]):
        send_ref[q] = empty
    slots = [(o, j) for o in (0, 2, 1) for j in range(peers)]
    packets = [
        jnp.concatenate(look_up(table, shared_ref[o, j : j + 1, :]), axis=1) for o, j in slots
    ]
    for (o, j), packet in zip(slots, packets):
        dom = jnp.clip(lax.axis_index("dom") + (o - 1), 0, doms - 1)
        for chip in range(2):
            send_ref[(dom * peers + j) * 2 + chip, :, : 2 * NN] = packet


def received_sums(shared_ref, recv_ref, *, doms, peers):
    indices = []
    values = []
    for o in range(3):
        dom = jnp.clip(lax.axis_index("dom") + (o - 1), 0, doms - 1)
        for j in range(peers):
            start = (dom * peers + j) * 2
            both = recv_ref[start] + recv_ref[start + 1]
            indices.append(shared_ref[o, j : j + 1, :])
            values.append([both[:, k * NN : (k + 1) * NN] for k in range(2)])
    total = None
    for at in range(0, len(indices), 8):
        part = spread(indices[at : at + 8], values[at : at + 8])
        total = part if total is None else total + part
    return to_fields(total)


def advance(base, mass, received):
    return [base[k] + mass * received[k] for k in range(2)]


def fill_base(base, current, previous, mass, own, other):
    for k in range(2):
        base[k] = 2.0 * current[k] - previous[k] + mass * (own[k] + other[k])


def base_kernel(ins, outs, scratch):
    own, other, mass, now0, now1, prev0, prev1 = (ref() for ref in ins[:7])
    current, previous = [now0[...], now1[...]], [prev0[...], prev1[...]]
    fill_base(outs[0], current, previous, mass[...], own, other)


def last_base_kernel(ins, outs, scratch):
    own, other, mass, current, now0, now1 = (ref() for ref in ins[:6])
    fill_base(outs[0], current, [now0[...], now1[...]], mass[...], own, other)


def drive_kernel(ins, outs, scratch):
    taps, signal = ins[0](), ins[-1]()
    (send,) = outs
    folded = []
    for t in range(2):
        products = taps[...] * signal[t : t + 1, :]
        products = sum(
            products[:, i * LANES : (i + 1) * LANES] for i in range(products.shape[1] // LANES)
        )
        folded.append(products[:, :64] + products[:, 64:])
    terms = jnp.concatenate(folded, axis=1)
    for q in range(send.shape[0]):
        send[q] = terms


def first_kernel(ins, outs, scratch):
    connect, now0, now1, surface, driver, metric, weights, narrow, narrow_back, wide = ins[:10]
    back, partial = outs
    vals, table = scratch
    fill_table(table, [now0()[...], now1()[...]])
    gather_all(table, connect(), vals)
    partial[...] = driver_sums(vals, surface(), driver_hot(driver()))
    operator(vals, metric, weights, narrow, narrow_back, wide, back)


def local_sums(res, connect, shared, partial, local, send, sums, table, sizes):
    scatter_all(res, connect, sums)
    fields = to_fields(sums[...])
    for k in range(2):
        local[k] = fields[k]
    local.flush()
    fill_table(table, fields)
    fill_send(table, shared, partial, send, **sizes)


def second_kernel(ins, outs, scratch, *, sizes):
    drive, surface, driver, back, connect, partial, shared = ins
    local, send = outs
    res, sums, table = scratch
    residual(amplitudes(0, drive(), driver_hot(driver())), surface(), back(), res)
    local_sums(res, connect(), shared(), partial()[...], local, send, sums, table, sizes)


def third_kernel(ins, outs, scratch, *, sizes):
    recv, base, mass, shared, connect, surface, driver, metric, weights, narrow, narrow_back, wide, drive = ins
    current, local, send = outs
    vals, back, res, sums, table = scratch
    received = received_sums(shared(), recv(), **sizes)
    fields = advance(base(), mass()[...], received)
    for k in range(2):
        current[k] = fields[k]
    current.flush()
    fill_table(table, fields)
    hot = driver_hot(driver())
    amplitude = amplitudes(1, drive(), hot)
    gather_all(table, connect(), vals)
    partial = driver_sums(vals, surface(), hot)
    operator(vals, metric, weights, narrow, narrow_back, wide, back)
    residual(amplitude, surface(), back, res)
    local_sums(res, connect(), shared(), partial, local, send, sums, table, sizes)


def last_kernel(ins, outs, scratch, *, sizes, scale):
    recv, base, mass, shared, recv_before, signal = ins
    out0, out1, grad = outs
    received = received_sums(shared(), recv(), **sizes)
    fields = advance(base(), mass()[...], received)
    for out, field in zip((out0, out1), fields):
        out[...] = field
        out.flush()

    def column(ref):
        row = sum(ref[q, :, 2 * NN :] for q in range(ref.shape[0]))
        ids = [lax.broadcasted_iota(jnp.int32, (8, LANES), axis) for axis in range(2)]
        row = jnp.where(ids[0] == ids[1], jnp.broadcast_to(row, (8, LANES)), 0.0)
        return jnp.sum(row, axis=1, keepdims=True) * scale

    window = signal()
    grad[...] = column(recv()) * window[0:1, :] + column(recv_before()) * window[1:2, :]


class Input:
    def __init__(self, source, buffer, semaphore):
        self.buffer = buffer
        self.copy = pltpu.make_async_copy(source, buffer, semaphore)
        self.waited = False
        self.copy.start()

    def __call__(self):
        if not self.waited:
            self.copy.wait()
            self.waited = True
        return self.buffer


class Output:
    def __init__(self, target, buffer, semaphore):
        self.buffer = buffer
        self.shape = buffer.shape
        self.copy = None if target is None else pltpu.make_async_copy(buffer, target, semaphore)
        self.sent = False

    def __setitem__(self, index, value):
        self.buffer[index] = value

    def flush(self):
        if self.copy is not None and not self.sent:
            self.copy.start()
            self.sent = True

    def wait(self):
        if self.copy is not None:
            self.copy.wait()


class Held:
    def __init__(self, value):
        self.value = value


ANY = pl.BlockSpec(memory_space=pl.ANY)
VMEM = pl.BlockSpec(memory_space=pltpu.VMEM)


def call(body, name, arrays, outs, scratch, window=None, held=(), keep=()):
    n_in, n_out = len(arrays), len(outs)
    fetched = [i for i, x in enumerate(arrays) if not isinstance(x, Held)]
    moved = [i for i in fetched if i not in keep]
    sent = [i for i in range(n_out) if i not in held]
    values = [
        pltpu.with_memory_space_constraint(x.value, pltpu.VMEM)
        if isinstance(x, Held)
        else pltpu.with_memory_space_constraint(x, pltpu.HBM)
        for x in arrays
    ]
    shapes = [x.shape for x in values]
    if window is not None:
        shapes[-1] = (shapes[-1][0], window)

    def kernel(*refs):
        sources, refs = list(refs[:n_in]), refs[n_in:]
        targets, refs = refs[:n_out], refs[n_out:]
        kept, refs = refs[: len(keep)], refs[len(keep) :]
        in_buffers, refs = refs[: len(moved)], refs[len(moved) :]
        out_buffers, refs = refs[: len(sent)], refs[len(sent) :]
        own, (in_sems, out_sems) = refs[:-2], refs[-2:]
        if window is not None:
            start = pl.multiple_of(lax.axis_index(ALL) * window, LANES)
            sources[-1] = sources[-1].at[:, pl.ds(start, window)]
        ins = [functools.partial(lambda ref: ref, ref) for ref in sources]
        buffers = dict(zip(moved, in_buffers)) | dict(zip(keep, kept))
        for at, i in enumerate(fetched):
            ins[i] = Input(sources[i], buffers[i], in_sems.at[at])
        results = [Output(None, ref, None) for ref in targets]
        for at, i in enumerate(sent):
            results[i] = Output(targets[i], out_buffers[at], out_sems.at[at])
        body(ins, results, own)
        for result in results:
            result.flush()
        for result in results:
            result.wait()
        for value in ins:
            value()

    results = pl.pallas_call(
        kernel,
        out_shape=[
            pltpu.VMEM(shape, F32) if i in held else jax.ShapeDtypeStruct(shape, F32)
            for i, shape in enumerate(outs)
        ]
        + [pltpu.VMEM(shapes[i], values[i].dtype) for i in keep],
        in_specs=[VMEM if isinstance(x, Held) else ANY for x in arrays],
        out_specs=[VMEM if i in held else ANY for i in range(n_out)] + [VMEM] * len(keep),
        scratch_shapes=[pltpu.VMEM(shapes[i], values[i].dtype) for i in moved]
        + [pltpu.VMEM(outs[i], F32) for i in sent]
        + [pltpu.VMEM(shape, dtype) for shape, dtype in scratch]
        + [
            pltpu.SemaphoreType.DMA((max(len(fetched), 1),)),
            pltpu.SemaphoreType.DMA((max(len(sent), 1),)),
        ],
        compiler_params=pltpu.CompilerParams(vmem_limit_bytes=40 << 20),
        name=name,
    )(*values)
    return [Held(x) if i in held or i >= n_out else x for i, x in enumerate(results)]


def on_device(
    field_prev,
    field_now,
    adjoint_now,
    adjoint_next,
    inv_mass,
    metric,
    connect,
    surface,
    driver,
    shared,
    filter_taps,
    signal,
):
    wide, narrow, narrow_back, weights = (jnp.asarray(t) for t in element_tables())
    count = connect.shape[0]
    peers = shared.shape[2]
    doms = lax.axis_size("dom")
    devices = lax.axis_size(ALL)
    width = filter_taps.shape[1]
    sizes = dict(doms=doms, peers=peers)
    plane = (LANES, LANES)
    now0, now1, prev0, prev1, mass = (
        x.reshape(plane) for x in (field_now, adjoint_now, field_prev, adjoint_next, inv_mass)
    )
    links = shared.reshape(3, peers, NN)
    driver_row = driver.reshape(1, count)
    if width % LANES == 0:
        window, taps, samples = width, filter_taps, signal
    else:
        window = None
        samples = lax.dynamic_slice_in_dim(signal, lax.axis_index(ALL) * width, width, 1)
        pad = ((0, 0), (0, -width % LANES))
        taps, samples = jnp.pad(filter_taps, pad), jnp.pad(samples, pad)

    def trade(x):
        return Held(lax.all_to_all(x.value, ALL, 0, 0, tiled=True))

    def swap(x):
        return Held(lax.ppermute(x.value, "chip", [(0, 1), (1, 0)]))

    nodes = (2,) + plane
    elements = ((2, count, NN), F32)
    sums = ((4 * ROWS, COLS), F32)
    table = ((4 * ROWS, COLS), BF)
    packet = (devices, 1, PACKET)
    terms, connect0, now0_held, now1_held = call(
        drive_kernel,
        "drive",
        [taps, connect, now0, now1, samples],
        [(devices, 8, LANES)],
        [],
        window,
        held=(0,),
        keep=(1, 2, 3),
    )
    drive = trade(terms)
    back, partial, surface0, driver0, links0 = call(
        first_kernel,
        "operator0",
        [connect0, now0_held, now1_held, surface, driver_row, metric, weights, narrow, narrow_back, wide, links],
        [elements[0], (1, LANES)],
        [elements, table],
        held=(0, 1),
        keep=(3, 4, 10),
    )
    local, send = call(
        functools.partial(second_kernel, sizes=sizes),
        "assemble0",
        [drive, surface0, driver0, back, connect0, partial, links0],
        [nodes, packet],
        [elements, sums, table],
        held=(0, 1),
    )
    other = swap(local)
    recv0 = trade(send)
    base, *rest = call(
        base_kernel,
        "base0",
        [local, other, mass, now0, now1, prev0, prev1, links, connect, surface, driver_row]
        + [metric, weights, narrow, narrow_back],
        [nodes],
        [],
        held=(0,),
        keep=(2, 7, 8, 9, 10, 11, 12, 13, 14),
    )
    current, local, send = call(
        functools.partial(third_kernel, sizes=sizes),
        "step1",
        [recv0, base, *rest, wide, drive],
        [nodes, nodes, packet],
        [elements, elements, elements, sums, table],
        held=(0, 1, 2),
    )
    other = swap(local)
    recv1 = trade(send)
    base, mass1, links1, samples1 = call(
        last_base_kernel,
        "base1",
        [local, other, mass, current, now0, now1, links, samples],
        [nodes],
        [],
        window,
        held=(0,),
        keep=(2, 6, 7),
    )
    out0, out1, grad = call(
        functools.partial(last_kernel, sizes=sizes, scale=1.0 / math.sqrt(NN * count * devices)),
        "finish",
        [recv1, base, mass1, links1, recv0, samples1],
        [plane, plane, (8, taps.shape[1])],
        [],
    )
    grad = grad[:, :width]
    return out0.reshape(1, -1), out1.reshape(1, -1), grad


def solution(mesh):
    region = P(("groups", "dom", "sub"), None)
    element = P(("groups", "dom", "sub", "chip"), None)
    in_specs = (
        region,
        region,
        region,
        region,
        region,
        element,
        element,
        element,
        P(("groups", "dom", "sub", "chip")),
        P(("groups", "dom", "sub"), None, None, None),
        P(None, ALL),
        P(),
    )
    out_specs = (region, region, P("groups", ALL))
    return jax.shard_map(
        on_device, mesh=mesh, in_specs=in_specs, out_specs=out_specs, check_vma=False
    )
```

```python
import functools
import math

import jax
import jax.numpy as jnp
import numpy as np
from jax import lax
from jax.experimental import pallas as pl
from jax.experimental.pallas import tpu as pltpu
from jax.sharding import PartitionSpec as P

NN = 512
LANES = 128
ROWS = 64
COLS = 256
BLOCK = 32
PACKET = 2 * NN + LANES
ALL = ("dom", "sub", "chip")

GLL_POINTS = (
    -1.0,
    -0.8717401485096066,
    -0.5917001814331423,
    -0.2092992179024789,
    0.2092992179024789,
    0.5917001814331423,
    0.8717401485096066,
    1.0,
)
GLL_WEIGHTS = (
    0.03571428571428571,
    0.21070422714350603,
    0.3411226924835044,
    0.4124587946587038,
    0.4124587946587038,
    0.3411226924835044,
    0.21070422714350603,
    0.03571428571428571,
)
BF = jnp.bfloat16
F32 = jnp.float32


def element_tables():
    points = np.array(GLL_POINTS)
    identity = np.eye(8)
    diffs = points[:, None] - points[None, :] + identity
    barycentric = 1.0 / np.prod(diffs, axis=1)
    derivative = barycentric[None, :] / barycentric[:, None] / diffs
    derivative = derivative * (1.0 - identity)
    derivative = derivative - identity * derivative.sum(axis=1)[:, None]
    along_x = np.kron(derivative, np.eye(64)).T
    along_y = np.kron(np.eye(4), np.kron(derivative, identity)).T
    along_z = np.kron(np.eye(32), derivative).T
    quad = np.array(GLL_WEIGHTS)
    cube = np.kron(np.kron(quad, quad), quad)

    def parts(table):
        table = table.astype(np.float32)
        high = table.astype(jnp.bfloat16)
        low = (table - high.astype(np.float32)).astype(jnp.bfloat16)
        return high, low

    wide = list(parts(along_x)) + list(parts(along_x.T))
    forward = parts(np.concatenate([along_y, along_z], axis=1))
    backward = parts(np.concatenate([along_y.T, along_z.T], axis=0))
    weights = np.concatenate([cube] * 3).astype(np.float32)[None, :]
    return np.stack(wide), np.stack(forward), np.stack(backward), weights


def halves(x):
    high = x.astype(BF)
    return high, (x - high.astype(F32)).astype(BF)


def mm(a, b):
    return jnp.dot(a, b, preferred_element_type=F32)


def times(x, high, low):
    xh, xl = halves(x)
    rows = x.shape[0]
    both = mm(jnp.concatenate([xh, xl], axis=0), high)
    return both[:rows] + both[rows:] + mm(xh, low)


def stack_halves(x):
    return jnp.concatenate([x[:, :256], x[:, 256:]], axis=0)


def unstack_halves(x):
    rows = x.shape[0] // 2
    return jnp.concatenate([x[:rows], x[rows:]], axis=1)


def split_index(index):
    row = (index >> 7) & (ROWS - 1)
    column = (index & (LANES - 1)) | ((index >> 13) << 7)
    return row, column


def column_hot(column):
    ids = lax.broadcasted_iota(jnp.int32, (COLS, NN), 0).astype(BF)
    return jnp.where(ids == column.astype(BF), BF(1), BF(0))


def fill_table(table_ref, fields):
    for k in range(2):
        field = fields[k]
        plane = jnp.concatenate([field[:ROWS], field[ROWS:]], axis=1)
        high, low = halves(plane)
        table_ref[k * ROWS : (k + 1) * ROWS] = high
        table_ref[(2 + k) * ROWS : (3 + k) * ROWS] = low


def look_up(table, index):
    row, column = split_index(index)
    found = mm(table, column_hot(column))
    found = found[: 2 * ROWS] + found[2 * ROWS :]
    mask = lax.broadcasted_iota(jnp.int32, (ROWS, NN), 0) == row
    return [
        jnp.sum(jnp.where(mask, found[k * ROWS : (k + 1) * ROWS], 0.0), axis=0, keepdims=True)
        for k in range(2)
    ]


def spread(indices, values):
    columns = []
    placed = []
    ids = lax.broadcasted_iota(jnp.int32, (ROWS, NN), 0).astype(BF)
    for index, pair in zip(indices, values):
        row, column = split_index(index)
        columns.append(column_hot(column))
        mask = ids == row.astype(BF)
        terms = [halves(v) for v in pair]
        placed.append(
            jnp.concatenate(
                [jnp.where(mask, terms[k][s], BF(0)) for s in range(2) for k in range(2)], axis=0
            )
        )
    left = jnp.concatenate(placed, axis=1) if len(placed) > 1 else placed[0]
    right = jnp.concatenate(columns, axis=1) if len(columns) > 1 else columns[0]
    return lax.dot_general(left, right, (((1,), (1,)), ((), ())), preferred_element_type=F32)


def to_fields(sums):
    sums = sums[: 2 * ROWS] + sums[2 * ROWS :]
    return [
        jnp.concatenate(
            [
                sums[k * ROWS : (k + 1) * ROWS, :LANES],
                sums[k * ROWS : (k + 1) * ROWS, LANES:],
            ],
            axis=0,
        )
        for k in range(2)
    ]


def gather_all(table_ref, connect_ref, vals_ref, row):
    count = connect_ref.shape[0]
    table = table_ref[...]
    last = count - 8
    passes = 2
    assert last % passes == 0
    block, rows = last // passes, LANES // passes
    blocks = range(NN // LANES)
    links = [connect_ref[last:, i * LANES : (i + 1) * LANES] for i in blocks]

    def body(i, found):
        found = list(found)
        done = 0
        for u in range(block):
            e = i * block + u
            pair = look_up(table, connect_ref[pl.ds(e, 1), :])
            for k in range(2):
                vals_ref[k, pl.ds(e, 1), :] = pair[k]
            upto = rows * (u + 1) // block
            for h in range(done, upto):
                node_row = i * rows + h
                for k in range(2):
                    values = jnp.broadcast_to(row(k, node_row), (8, LANES))
                    for n in blocks:
                        picked = jnp.take_along_axis(
                            values, links[n] & (LANES - 1), axis=1, mode="promise_in_bounds"
                        )
                        at = 2 * n + k
                        found[at] = jnp.where((links[n] >> 7) == node_row, picked, found[at])
            done = upto
        return tuple(found)

    found = lax.fori_loop(0, passes, body, (jnp.zeros((8, LANES), F32),) * (2 * len(blocks)))
    for n in blocks:
        for k in range(2):
            vals_ref[k, last:, n * LANES : (n + 1) * LANES] = found[2 * n + k]


def operator(vals_ref, metric, weights, narrow, narrow_back, wide, back_ref):
    count = vals_ref.shape[1]
    vals = jnp.concatenate([vals_ref[0], vals_ref[1]], axis=0)
    scale = metric()[...] * weights()[...]
    scale = jnp.concatenate([scale, scale], axis=0)
    along = [scale[:, i * NN : (i + 1) * NN] for i in range(3)]
    table = narrow()
    grads = times(stack_halves(vals), table[0], table[1])
    grads = grads * jnp.concatenate([stack_halves(x) for x in along[1:]], axis=1)
    table = narrow_back()
    total = unstack_halves(times(grads, table[0], table[1]))
    table = wide()
    total += times(times(vals, table[0], table[1]) * along[0], table[2], table[3])
    back_ref[0] = total[:count]
    back_ref[1] = total[count:]


def driver_hot(driver_ref):
    count = driver_ref.shape[1]
    ids = lax.broadcasted_iota(jnp.int32, (LANES, count), 0)
    return ((ids == driver_ref[...]) & (ids < 8)).astype(F32).T


def driver_sums(vals_ref, surface_ref, hot):
    products = surface_ref[...] * vals_ref[1]
    products = sum(products[:, i * LANES : (i + 1) * LANES] for i in range(NN // LANES))
    return jnp.sum(hot * jnp.sum(products, axis=1, keepdims=True), axis=0, keepdims=True)


def amplitudes(step, drive_ref, hot):
    terms = jnp.sum(drive_ref[...], axis=0)
    half = lax.broadcasted_iota(jnp.int32, (8, LANES), 1) >> 6
    drive = jnp.sum(jnp.where(half == step, terms, 0.0), axis=1, keepdims=True)
    ids = [lax.broadcasted_iota(jnp.int32, (8, LANES), axis) for axis in range(2)]
    row = jnp.sum(jnp.where(ids[0] == ids[1], drive, 0.0), axis=0, keepdims=True)
    return jnp.sum(hot * row, axis=1, keepdims=True)


def residual(amplitude, surface_ref, back_ref, res_ref):
    res_ref[0] = amplitude * surface_ref[...] - back_ref[0]
    res_ref[1] = -back_ref[1]


def scatter_all(res_ref, connect_ref, sums_ref):
    count = connect_ref.shape[0]

    def part(i):
        rows = [pl.ds(i * BLOCK + u, 1) for u in range(BLOCK)]
        return spread(
            [connect_ref[r, :] for r in rows],
            [[res_ref[k, r, :] for k in range(2)] for r in rows],
        )

    if count == BLOCK:
        sums_ref[...] = part(0)
        return
    sums_ref[...] = jnp.zeros_like(sums_ref)

    def body(i, carry):
        sums_ref[...] += part(i)
        return carry

    lax.fori_loop(0, count // BLOCK, body, 0)


def fill_send(table_ref, shared_ref, partial, send_ref, *, doms, peers):
    table = table_ref[...]
    empty = jnp.concatenate([jnp.zeros((1, 2 * NN), F32), partial], axis=1)
    for q in range(send_ref.shape[0]):
        send_ref[q] = empty
    slots = [(o, j) for o in (0, 2, 1) for j in range(peers)]
    packets = [
        jnp.concatenate(look_up(table, shared_ref[o, j : j + 1, :]), axis=1) for o, j in slots
    ]
    for (o, j), packet in zip(slots, packets):
        dom = jnp.clip(lax.axis_index("dom") + (o - 1), 0, doms - 1)
        for chip in range(2):
            send_ref[(dom * peers + j) * 2 + chip, :, : 2 * NN] = packet


def received_sums(shared_ref, recv_ref, *, doms, peers):
    indices = []
    values = []
    for o in range(3):
        dom = jnp.clip(lax.axis_index("dom") + (o - 1), 0, doms - 1)
        for j in range(peers):
            start = (dom * peers + j) * 2
            both = recv_ref[start] + recv_ref[start + 1]
            indices.append(shared_ref[o, j : j + 1, :])
            values.append([both[:, k * NN : (k + 1) * NN] for k in range(2)])
    total = None
    for at in range(0, len(indices), 8):
        part = spread(indices[at : at + 8], values[at : at + 8])
        total = part if total is None else total + part
    return to_fields(total)


def advance(base, mass, received):
    return [base[k] + mass * received[k] for k in range(2)]


def fill_base(base, current, previous, mass, own, other):
    for k in range(2):
        base[k] = 2.0 * current[k] - previous[k] + mass * (own[k] + other[k])


def base_kernel(ins, outs, scratch):
    own, other, mass, now0, now1, prev0, prev1 = (ref() for ref in ins[:7])
    current, previous = [now0[...], now1[...]], [prev0[...], prev1[...]]
    fill_base(outs[0], current, previous, mass[...], own, other)


def last_base_kernel(ins, outs, scratch):
    own, other, mass, current, now0, now1 = (ref() for ref in ins[:6])
    fill_base(outs[0], current, [now0[...], now1[...]], mass[...], own, other)


def drive_kernel(ins, outs, scratch):
    taps, signal = ins[0](), ins[-1]()
    (send,) = outs
    folded = []
    for t in range(2):
        products = taps[...] * signal[t : t + 1, :]
        products = sum(
            products[:, i * LANES : (i + 1) * LANES] for i in range(products.shape[1] // LANES)
        )
        folded.append(products[:, :64] + products[:, 64:])
    terms = jnp.concatenate(folded, axis=1)
    for q in range(send.shape[0]):
        send[q] = terms


def first_kernel(ins, outs, scratch):
    connect, now0, now1, surface, driver, metric, weights, narrow, narrow_back, wide = ins[:10]
    back, partial = outs
    vals, table = scratch
    fill_table(table, [now0()[...], now1()[...]])
    now = (now0(), now1())
    gather_all(table, connect(), vals, lambda k, r: now[k][pl.ds(r, 1), :])
    partial[...] = driver_sums(vals, surface(), driver_hot(driver()))
    operator(vals, metric, weights, narrow, narrow_back, wide, back)


def local_sums(res, connect, shared, partial, local, send, sums, table, sizes):
    scatter_all(res, connect, sums)
    fields = to_fields(sums[...])
    for k in range(2):
        local[k] = fields[k]
    local.flush()
    fill_table(table, fields)
    fill_send(table, shared, partial, send, **sizes)


def second_kernel(ins, outs, scratch, *, sizes):
    drive, surface, driver, back, connect, partial, shared = ins
    local, send = outs
    res, sums, table = scratch
    residual(amplitudes(0, drive(), driver_hot(driver())), surface(), back(), res)
    local_sums(res, connect(), shared(), partial()[...], local, send, sums, table, sizes)


def third_kernel(ins, outs, scratch, *, sizes):
    recv, base, mass, shared, connect, surface, driver, metric, weights, narrow, narrow_back, wide, drive = ins
    current, local, send = outs
    vals, back, res, sums, table = scratch
    received = received_sums(shared(), recv(), **sizes)
    fields = advance(base(), mass()[...], received)
    for k in range(2):
        current[k] = fields[k]
    current.flush()
    fill_table(table, fields)
    hot = driver_hot(driver())
    amplitude = amplitudes(1, drive(), hot)
    gather_all(table, connect(), vals, lambda k, r: current.buffer[k, pl.ds(r, 1), :])
    partial = driver_sums(vals, surface(), hot)
    operator(vals, metric, weights, narrow, narrow_back, wide, back)
    residual(amplitude, surface(), back, res)
    local_sums(res, connect(), shared(), partial, local, send, sums, table, sizes)


def last_kernel(ins, outs, scratch, *, sizes, scale):
    recv, base, mass, shared, recv_before, signal = ins
    out0, out1, grad = outs
    received = received_sums(shared(), recv(), **sizes)
    fields = advance(base(), mass()[...], received)
    for out, field in zip((out0, out1), fields):
        out[...] = field
        out.flush()

    def column(ref):
        row = sum(ref[q, :, 2 * NN :] for q in range(ref.shape[0]))
        ids = [lax.broadcasted_iota(jnp.int32, (8, LANES), axis) for axis in range(2)]
        row = jnp.where(ids[0] == ids[1], jnp.broadcast_to(row, (8, LANES)), 0.0)
        return jnp.sum(row, axis=1, keepdims=True) * scale

    window = signal()
    grad[...] = column(recv()) * window[0:1, :] + column(recv_before()) * window[1:2, :]


class Input:
    def __init__(self, source, buffer, semaphore):
        self.buffer = buffer
        self.copy = pltpu.make_async_copy(source, buffer, semaphore)
        self.waited = False
        self.copy.start()

    def __call__(self):
        if not self.waited:
            self.copy.wait()
            self.waited = True
        return self.buffer


class Output:
    def __init__(self, target, buffer, semaphore):
        self.buffer = buffer
        self.shape = buffer.shape
        self.copy = None if target is None else pltpu.make_async_copy(buffer, target, semaphore)
        self.sent = False

    def __setitem__(self, index, value):
        self.buffer[index] = value

    def flush(self):
        if self.copy is not None and not self.sent:
            self.copy.start()
            self.sent = True

    def wait(self):
        if self.copy is not None:
            self.copy.wait()


class Held:
    def __init__(self, value):
        self.value = value


ANY = pl.BlockSpec(memory_space=pl.ANY)
VMEM = pl.BlockSpec(memory_space=pltpu.VMEM)


def call(body, name, arrays, outs, scratch, window=None, held=(), keep=()):
    n_in, n_out = len(arrays), len(outs)
    fetched = [i for i, x in enumerate(arrays) if not isinstance(x, Held)]
    moved = [i for i in fetched if i not in keep]
    sent = [i for i in range(n_out) if i not in held]
    values = [
        pltpu.with_memory_space_constraint(x.value, pltpu.VMEM)
        if isinstance(x, Held)
        else pltpu.with_memory_space_constraint(x, pltpu.HBM)
        for x in arrays
    ]
    shapes = [x.shape for x in values]
    if window is not None:
        shapes[-1] = (shapes[-1][0], window)

    def kernel(*refs):
        sources, refs = list(refs[:n_in]), refs[n_in:]
        targets, refs = refs[:n_out], refs[n_out:]
        kept, refs = refs[: len(keep)], refs[len(keep) :]
        in_buffers, refs = refs[: len(moved)], refs[len(moved) :]
        out_buffers, refs = refs[: len(sent)], refs[len(sent) :]
        own, (in_sems, out_sems) = refs[:-2], refs[-2:]
        if window is not None:
            start = pl.multiple_of(lax.axis_index(ALL) * window, LANES)
            sources[-1] = sources[-1].at[:, pl.ds(start, window)]
        ins = [functools.partial(lambda ref: ref, ref) for ref in sources]
        buffers = dict(zip(moved, in_buffers)) | dict(zip(keep, kept))
        for at, i in enumerate(fetched):
            ins[i] = Input(sources[i], buffers[i], in_sems.at[at])
        results = [Output(None, ref, None) for ref in targets]
        for at, i in enumerate(sent):
            results[i] = Output(targets[i], out_buffers[at], out_sems.at[at])
        body(ins, results, own)
        for result in results:
            result.flush()
        for result in results:
            result.wait()
        for value in ins:
            value()

    results = pl.pallas_call(
        kernel,
        out_shape=[
            pltpu.VMEM(shape, F32) if i in held else jax.ShapeDtypeStruct(shape, F32)
            for i, shape in enumerate(outs)
        ]
        + [pltpu.VMEM(shapes[i], values[i].dtype) for i in keep],
        in_specs=[VMEM if isinstance(x, Held) else ANY for x in arrays],
        out_specs=[VMEM if i in held else ANY for i in range(n_out)] + [VMEM] * len(keep),
        scratch_shapes=[pltpu.VMEM(shapes[i], values[i].dtype) for i in moved]
        + [pltpu.VMEM(outs[i], F32) for i in sent]
        + [pltpu.VMEM(shape, dtype) for shape, dtype in scratch]
        + [
            pltpu.SemaphoreType.DMA((max(len(fetched), 1),)),
            pltpu.SemaphoreType.DMA((max(len(sent), 1),)),
        ],
        compiler_params=pltpu.CompilerParams(vmem_limit_bytes=40 << 20),
        name=name,
    )(*values)
    return [Held(x) if i in held or i >= n_out else x for i, x in enumerate(results)]


def on_device(
    field_prev,
    field_now,
    adjoint_now,
    adjoint_next,
    inv_mass,
    metric,
    connect,
    surface,
    driver,
    shared,
    filter_taps,
    signal,
):
    wide, narrow, narrow_back, weights = (jnp.asarray(t) for t in element_tables())
    count = connect.shape[0]
    peers = shared.shape[2]
    doms = lax.axis_size("dom")
    devices = lax.axis_size(ALL)
    width = filter_taps.shape[1]
    sizes = dict(doms=doms, peers=peers)
    plane = (LANES, LANES)
    now0, now1, prev0, prev1, mass = (
        x.reshape(plane) for x in (field_now, adjoint_now, field_prev, adjoint_next, inv_mass)
    )
    links = shared.reshape(3, peers, NN)
    driver_row = driver.reshape(1, count)
    if width % LANES == 0:
        window, taps, samples = width, filter_taps, signal
    else:
        window = None
        samples = lax.dynamic_slice_in_dim(signal, lax.axis_index(ALL) * width, width, 1)
        pad = ((0, 0), (0, -width % LANES))
        taps, samples = jnp.pad(filter_taps, pad), jnp.pad(samples, pad)

    def trade(x):
        return Held(lax.all_to_all(x.value, ALL, 0, 0, tiled=True))

    def swap(x):
        return Held(lax.ppermute(x.value, "chip", [(0, 1), (1, 0)]))

    nodes = (2,) + plane
    elements = ((2, count, NN), F32)
    sums = ((4 * ROWS, COLS), F32)
    table = ((4 * ROWS, COLS), BF)
    packet = (devices, 1, PACKET)
    terms, connect0, now0_held, now1_held = call(
        drive_kernel,
        "drive",
        [taps, connect, now0, now1, samples],
        [(devices, 8, LANES)],
        [],
        window,
        held=(0,),
        keep=(1, 2, 3),
    )
    drive = trade(terms)
    back, partial, surface0, driver0, links0 = call(
        first_kernel,
        "operator0",
        [connect0, now0_held, now1_held, surface, driver_row, metric, weights, narrow, narrow_back, wide, links],
        [elements[0], (1, LANES)],
        [elements, table],
        held=(0, 1),
        keep=(3, 4, 10),
    )
    local, send = call(
        functools.partial(second_kernel, sizes=sizes),
        "assemble0",
        [drive, surface0, driver0, back, connect0, partial, links0],
        [nodes, packet],
        [elements, sums, table],
        held=(0, 1),
    )
    other = swap(local)
    recv0 = trade(send)
    base, *rest = call(
        base_kernel,
        "base0",
        [local, other, mass, now0, now1, prev0, prev1, links, connect, surface, driver_row]
        + [metric, weights, narrow, narrow_back],
        [nodes],
        [],
        held=(0,),
        keep=(2, 7, 8, 9, 10, 11, 12, 13, 14),
    )
    current, local, send = call(
        functools.partial(third_kernel, sizes=sizes),
        "step1",
        [recv0, base, *rest, wide, drive],
        [nodes, nodes, packet],
        [elements, elements, elements, sums, table],
        held=(0, 1, 2),
    )
    other = swap(local)
    recv1 = trade(send)
    base, mass1, links1, samples1 = call(
        last_base_kernel,
        "base1",
        [local, other, mass, current, now0, now1, links, samples],
        [nodes],
        [],
        window,
        held=(0,),
        keep=(2, 6, 7),
    )
    out0, out1, grad = call(
        functools.partial(last_kernel, sizes=sizes, scale=1.0 / math.sqrt(NN * count * devices)),
        "finish",
        [recv1, base, mass1, links1, recv0, samples1],
        [plane, plane, (8, taps.shape[1])],
        [],
    )
    grad = grad[:, :width]
    return out0.reshape(1, -1), out1.reshape(1, -1), grad


def solution(mesh):
    region = P(("groups", "dom", "sub"), None)
    element = P(("groups", "dom", "sub", "chip"), None)
    in_specs = (
        region,
        region,
        region,
        region,
        region,
        element,
        element,
        element,
        P(("groups", "dom", "sub", "chip")),
        P(("groups", "dom", "sub"), None, None, None),
        P(None, ALL),
        P(),
    )
    out_specs = (region, region, P("groups", ALL))
    return jax.shard_map(
        on_device, mesh=mesh, in_specs=in_specs, out_specs=out_specs, check_vma=False
    )
```

```python
import functools
import math

import jax
import jax.numpy as jnp
import numpy as np
from jax import lax
from jax.experimental import pallas as pl
from jax.experimental.pallas import tpu as pltpu
from jax.sharding import PartitionSpec as P

NN = 512
LANES = 128
ROWS = 64
COLS = 256
BLOCK = 32
PACKET = 2 * NN + LANES
ALL = ("dom", "sub", "chip")

GLL_POINTS = (
    -1.0,
    -0.8717401485096066,
    -0.5917001814331423,
    -0.2092992179024789,
    0.2092992179024789,
    0.5917001814331423,
    0.8717401485096066,
    1.0,
)
GLL_WEIGHTS = (
    0.03571428571428571,
    0.21070422714350603,
    0.3411226924835044,
    0.4124587946587038,
    0.4124587946587038,
    0.3411226924835044,
    0.21070422714350603,
    0.03571428571428571,
)
BF = jnp.bfloat16
F32 = jnp.float32


def element_tables():
    points = np.array(GLL_POINTS)
    identity = np.eye(8)
    diffs = points[:, None] - points[None, :] + identity
    barycentric = 1.0 / np.prod(diffs, axis=1)
    derivative = barycentric[None, :] / barycentric[:, None] / diffs
    derivative = derivative * (1.0 - identity)
    derivative = derivative - identity * derivative.sum(axis=1)[:, None]
    along_x = np.kron(derivative, np.eye(64)).T
    along_y = np.kron(np.eye(4), np.kron(derivative, identity)).T
    along_z = np.kron(np.eye(32), derivative).T
    quad = np.array(GLL_WEIGHTS)
    cube = np.kron(np.kron(quad, quad), quad)

    def parts(table):
        table = table.astype(np.float32)
        high = table.astype(jnp.bfloat16)
        low = (table - high.astype(np.float32)).astype(jnp.bfloat16)
        return high, low

    wide = list(parts(along_x)) + list(parts(along_x.T))
    forward = parts(np.concatenate([along_y, along_z], axis=1))
    backward = parts(np.concatenate([along_y.T, along_z.T], axis=0))
    weights = np.concatenate([cube] * 3).astype(np.float32)[None, :]
    return np.stack(wide), np.stack(forward), np.stack(backward), weights


def halves(x):
    high = x.astype(BF)
    return high, (x - high.astype(F32)).astype(BF)


def mm(a, b):
    return jnp.dot(a, b, preferred_element_type=F32)


def times(x, high, low):
    xh, xl = halves(x)
    rows = x.shape[0]
    both = mm(jnp.concatenate([xh, xl], axis=0), high)
    return both[:rows] + both[rows:] + mm(xh, low)


def stack_halves(x):
    return jnp.concatenate([x[:, :256], x[:, 256:]], axis=0)


def unstack_halves(x):
    rows = x.shape[0] // 2
    return jnp.concatenate([x[:rows], x[rows:]], axis=1)


def split_index(index):
    row = (index >> 7) & (ROWS - 1)
    column = (index & (LANES - 1)) | ((index >> 13) << 7)
    return row, column


def column_hot(column):
    ids = lax.broadcasted_iota(jnp.int32, (COLS, NN), 0).astype(BF)
    return jnp.where(ids == column.astype(BF), BF(1), BF(0))


def fill_table(table_ref, fields):
    for k in range(2):
        field = fields[k]
        plane = jnp.concatenate([field[:ROWS], field[ROWS:]], axis=1)
        high, low = halves(plane)
        table_ref[k * ROWS : (k + 1) * ROWS] = high
        table_ref[(2 + k) * ROWS : (3 + k) * ROWS] = low


def look_up_columns(table, index):
    row, column = split_index(index)
    return mm(table, column_hot(column)), row


def pick_rows(found, row):
    found = found[: 2 * ROWS] + found[2 * ROWS :]
    mask = lax.broadcasted_iota(jnp.int32, (ROWS, NN), 0) == row
    return [
        jnp.sum(jnp.where(mask, found[k * ROWS : (k + 1) * ROWS], 0.0), axis=0, keepdims=True)
        for k in range(2)
    ]


def spread(indices, values):
    columns = []
    placed = []
    ids = lax.broadcasted_iota(jnp.int32, (ROWS, NN), 0).astype(BF)
    for index, pair in zip(indices, values):
        row, column = split_index(index)
        columns.append(column_hot(column))
        mask = ids == row.astype(BF)
        terms = [halves(v) for v in pair]
        placed.append(
            jnp.concatenate(
                [jnp.where(mask, terms[k][s], BF(0)) for s in range(2) for k in range(2)], axis=0
            )
        )
    left = jnp.concatenate(placed, axis=1) if len(placed) > 1 else placed[0]
    right = jnp.concatenate(columns, axis=1) if len(columns) > 1 else columns[0]
    return lax.dot_general(left, right, (((1,), (1,)), ((), ())), preferred_element_type=F32)


def to_fields(sums):
    sums = sums[: 2 * ROWS] + sums[2 * ROWS :]
    return [
        jnp.concatenate(
            [
                sums[k * ROWS : (k + 1) * ROWS, :LANES],
                sums[k * ROWS : (k + 1) * ROWS, LANES:],
            ],
            axis=0,
        )
        for k in range(2)
    ]


def gather_all(table_ref, connect_ref, vals_ref, row):
    count = connect_ref.shape[0]
    table = table_ref[...]
    last = count - 8
    passes = 2
    assert last % passes == 0
    block, rows = last // passes, LANES // passes
    blocks = range(NN // LANES)
    links = [connect_ref[last:, i * LANES : (i + 1) * LANES] for i in blocks]

    def store(e, columns):
        pair = pick_rows(*columns)
        for k in range(2):
            vals_ref[k, pl.ds(e, 1), :] = pair[k]

    def body(i, found):
        found = list(found)
        done = 0
        columns = None
        for u in range(block):
            e = i * block + u
            before = columns
            columns = look_up_columns(table, connect_ref[pl.ds(e, 1), :])
            if before is not None:
                store(e - 1, before)
            upto = rows * (u + 1) // block
            for h in range(done, upto):
                node_row = i * rows + h
                for k in range(2):
                    values = jnp.broadcast_to(row(k, node_row), (8, LANES))
                    for n in blocks:
                        picked = jnp.take_along_axis(
                            values, links[n] & (LANES - 1), axis=1, mode="promise_in_bounds"
                        )
                        at = 2 * n + k
                        found[at] = jnp.where((links[n] >> 7) == node_row, picked, found[at])
            done = upto
        store(i * block + block - 1, columns)
        return tuple(found)

    found = lax.fori_loop(0, passes, body, (jnp.zeros((8, LANES), F32),) * (2 * len(blocks)))
    for n in blocks:
        for k in range(2):
            vals_ref[k, last:, n * LANES : (n + 1) * LANES] = found[2 * n + k]


def operator(vals_ref, metric, weights, narrow, narrow_back, wide, back_ref):
    count = vals_ref.shape[1]
    vals = jnp.concatenate([vals_ref[0], vals_ref[1]], axis=0)
    scale = metric()[...] * weights()[...]
    scale = jnp.concatenate([scale, scale], axis=0)
    along = [scale[:, i * NN : (i + 1) * NN] for i in range(3)]
    split, across, table = narrow(), narrow_back(), wide()
    grads = times(stack_halves(vals), split[0], split[1])
    along_x = times(vals, table[0], table[1])
    grads = grads * jnp.concatenate([stack_halves(x) for x in along[1:]], axis=1)
    along_x = along_x * along[0]
    total = unstack_halves(times(grads, across[0], across[1]))
    total += times(along_x, table[2], table[3])
    back_ref[0] = total[:count]
    back_ref[1] = total[count:]


def driver_hot(driver_ref):
    count = driver_ref.shape[1]
    ids = lax.broadcasted_iota(jnp.int32, (LANES, count), 0)
    return ((ids == driver_ref[...]) & (ids < 8)).astype(F32).T


def driver_sums(vals_ref, surface_ref, hot):
    products = surface_ref[...] * vals_ref[1]
    products = sum(products[:, i * LANES : (i + 1) * LANES] for i in range(NN // LANES))
    return jnp.sum(hot * jnp.sum(products, axis=1, keepdims=True), axis=0, keepdims=True)


def amplitudes(step, drive_ref, hot):
    terms = jnp.sum(drive_ref[...], axis=0)
    half = lax.broadcasted_iota(jnp.int32, (8, LANES), 1) >> 6
    drive = jnp.sum(jnp.where(half == step, terms, 0.0), axis=1, keepdims=True)
    ids = [lax.broadcasted_iota(jnp.int32, (8, LANES), axis) for axis in range(2)]
    row = jnp.sum(jnp.where(ids[0] == ids[1], drive, 0.0), axis=0, keepdims=True)
    return jnp.sum(hot * row, axis=1, keepdims=True)


def residual(amplitude, surface_ref, back_ref, res_ref):
    res_ref[0] = amplitude * surface_ref[...] - back_ref[0]
    res_ref[1] = -back_ref[1]


def scatter_all(res_ref, connect_ref, sums_ref):
    count = connect_ref.shape[0]

    def part(i):
        rows = [pl.ds(i * BLOCK + u, 1) for u in range(BLOCK)]
        return spread(
            [connect_ref[r, :] for r in rows],
            [[res_ref[k, r, :] for k in range(2)] for r in rows],
        )

    if count == BLOCK:
        sums_ref[...] = part(0)
        return
    sums_ref[...] = jnp.zeros_like(sums_ref)

    def body(i, carry):
        sums_ref[...] += part(i)
        return carry

    lax.fori_loop(0, count // BLOCK, body, 0)


def fill_send(table_ref, shared_ref, partial, send_ref, *, doms, peers):
    table = table_ref[...]
    empty = jnp.concatenate([jnp.zeros((1, 2 * NN), F32), partial], axis=1)
    for q in range(send_ref.shape[0]):
        send_ref[q] = empty
    slots = [(o, j) for o in (0, 2, 1) for j in range(peers)]
    columns = [look_up_columns(table, shared_ref[o, j : j + 1, :]) for o, j in slots]
    packets = [jnp.concatenate(pick_rows(*found), axis=1) for found in columns]
    for (o, j), packet in zip(slots, packets):
        dom = jnp.clip(lax.axis_index("dom") + (o - 1), 0, doms - 1)
        for chip in range(2):
            send_ref[(dom * peers + j) * 2 + chip, :, : 2 * NN] = packet


def received_sums(shared_ref, recv_ref, *, doms, peers):
    indices = []
    values = []
    for o in range(3):
        dom = jnp.clip(lax.axis_index("dom") + (o - 1), 0, doms - 1)
        for j in range(peers):
            start = (dom * peers + j) * 2
            both = recv_ref[start] + recv_ref[start + 1]
            indices.append(shared_ref[o, j : j + 1, :])
            values.append([both[:, k * NN : (k + 1) * NN] for k in range(2)])
    total = None
    for at in range(0, len(indices), 8):
        part = spread(indices[at : at + 8], values[at : at + 8])
        total = part if total is None else total + part
    return to_fields(total)


def advance(base, mass, received):
    return [base[k] + mass * received[k] for k in range(2)]


def fill_base(base, current, previous, mass, own, other):
    for k in range(2):
        base[k] = 2.0 * current[k] - previous[k] + mass * (own[k] + other[k])


def base_kernel(ins, outs, scratch):
    own, other, mass, now0, now1, prev0, prev1 = (ref() for ref in ins[:7])
    current, previous = [now0[...], now1[...]], [prev0[...], prev1[...]]
    fill_base(outs[0], current, previous, mass[...], own, other)


def last_base_kernel(ins, outs, scratch):
    own, other, mass, current, now0, now1 = (ref() for ref in ins[:6])
    fill_base(outs[0], current, [now0[...], now1[...]], mass[...], own, other)


def drive_kernel(ins, outs, scratch):
    taps, signal = ins[0](), ins[-1]()
    (send,) = outs
    folded = []
    for t in range(2):
        products = taps[...] * signal[t : t + 1, :]
        products = sum(
            products[:, i * LANES : (i + 1) * LANES] for i in range(products.shape[1] // LANES)
        )
        folded.append(products[:, :64] + products[:, 64:])
    terms = jnp.concatenate(folded, axis=1)
    for q in range(send.shape[0]):
        send[q] = terms


def first_kernel(ins, outs, scratch):
    connect, now0, now1, surface, driver, metric, weights, narrow, narrow_back, wide = ins[:10]
    back, partial = outs
    vals, table = scratch
    fill_table(table, [now0()[...], now1()[...]])
    now = (now0(), now1())
    gather_all(table, connect(), vals, lambda k, r: now[k][pl.ds(r, 1), :])
    partial[...] = driver_sums(vals, surface(), driver_hot(driver()))
    operator(vals, metric, weights, narrow, narrow_back, wide, back)


def local_sums(res, connect, shared, partial, local, send, sums, table, sizes):
    scatter_all(res, connect, sums)
    fields = to_fields(sums[...])
    for k in range(2):
        local[k] = fields[k]
    local.flush()
    fill_table(table, fields)
    fill_send(table, shared, partial, send, **sizes)


def second_kernel(ins, outs, scratch, *, sizes):
    drive, surface, driver, back, connect, partial, shared = ins
    local, send = outs
    res, sums, table = scratch
    residual(amplitudes(0, drive(), driver_hot(driver())), surface(), back(), res)
    local_sums(res, connect(), shared(), partial()[...], local, send, sums, table, sizes)


def third_kernel(ins, outs, scratch, *, sizes):
    recv, base, mass, shared, connect, surface, driver, metric, weights, narrow, narrow_back, wide, drive = ins
    current, local, send = outs
    vals, back, res, sums, table = scratch
    received = received_sums(shared(), recv(), **sizes)
    fields = advance(base(), mass()[...], received)
    for k in range(2):
        current[k] = fields[k]
    current.flush()
    fill_table(table, fields)
    hot = driver_hot(driver())
    amplitude = amplitudes(1, drive(), hot)
    gather_all(table, connect(), vals, lambda k, r: current.buffer[k, pl.ds(r, 1), :])
    partial = driver_sums(vals, surface(), hot)
    operator(vals, metric, weights, narrow, narrow_back, wide, back)
    residual(amplitude, surface(), back, res)
    local_sums(res, connect(), shared(), partial, local, send, sums, table, sizes)


def last_kernel(ins, outs, scratch, *, sizes, scale):
    recv, base, mass, shared, recv_before, signal = ins
    out0, out1, grad = outs
    received = received_sums(shared(), recv(), **sizes)
    fields = advance(base(), mass()[...], received)
    for out, field in zip((out0, out1), fields):
        out[...] = field
        out.flush()

    def column(ref):
        row = sum(ref[q, :, 2 * NN :] for q in range(ref.shape[0]))
        ids = [lax.broadcasted_iota(jnp.int32, (8, LANES), axis) for axis in range(2)]
        row = jnp.where(ids[0] == ids[1], jnp.broadcast_to(row, (8, LANES)), 0.0)
        return jnp.sum(row, axis=1, keepdims=True) * scale

    window = signal()
    grad[...] = column(recv()) * window[0:1, :] + column(recv_before()) * window[1:2, :]


class Input:
    def __init__(self, source, buffer, semaphore):
        self.buffer = buffer
        self.copy = pltpu.make_async_copy(source, buffer, semaphore)
        self.waited = False
        self.copy.start()

    def __call__(self):
        if not self.waited:
            self.copy.wait()
            self.waited = True
        return self.buffer


class Output:
    def __init__(self, target, buffer, semaphore):
        self.buffer = buffer
        self.shape = buffer.shape
        self.copy = None if target is None else pltpu.make_async_copy(buffer, target, semaphore)
        self.sent = False

    def __setitem__(self, index, value):
        self.buffer[index] = value

    def flush(self):
        if self.copy is not None and not self.sent:
            self.copy.start()
            self.sent = True

    def wait(self):
        if self.copy is not None:
            self.copy.wait()


class Held:
    def __init__(self, value):
        self.value = value


ANY = pl.BlockSpec(memory_space=pl.ANY)
VMEM = pl.BlockSpec(memory_space=pltpu.VMEM)


def call(body, name, arrays, outs, scratch, window=None, held=(), keep=()):
    n_in, n_out = len(arrays), len(outs)
    fetched = [i for i, x in enumerate(arrays) if not isinstance(x, Held)]
    moved = [i for i in fetched if i not in keep]
    sent = [i for i in range(n_out) if i not in held]
    values = [
        pltpu.with_memory_space_constraint(x.value, pltpu.VMEM)
        if isinstance(x, Held)
        else pltpu.with_memory_space_constraint(x, pltpu.HBM)
        for x in arrays
    ]
    shapes = [x.shape for x in values]
    if window is not None:
        shapes[-1] = (shapes[-1][0], window)

    def kernel(*refs):
        sources, refs = list(refs[:n_in]), refs[n_in:]
        targets, refs = refs[:n_out], refs[n_out:]
        kept, refs = refs[: len(keep)], refs[len(keep) :]
        in_buffers, refs = refs[: len(moved)], refs[len(moved) :]
        out_buffers, refs = refs[: len(sent)], refs[len(sent) :]
        own, (in_sems, out_sems) = refs[:-2], refs[-2:]
        if window is not None:
            start = pl.multiple_of(lax.axis_index(ALL) * window, LANES)
            sources[-1] = sources[-1].at[:, pl.ds(start, window)]
        ins = [functools.partial(lambda ref: ref, ref) for ref in sources]
        buffers = dict(zip(moved, in_buffers)) | dict(zip(keep, kept))
        for at, i in enumerate(fetched):
            ins[i] = Input(sources[i], buffers[i], in_sems.at[at])
        results = [Output(None, ref, None) for ref in targets]
        for at, i in enumerate(sent):
            results[i] = Output(targets[i], out_buffers[at], out_sems.at[at])
        body(ins, results, own)
        for result in results:
            result.flush()
        for result in results:
            result.wait()
        for value in ins:
            value()

    results = pl.pallas_call(
        kernel,
        out_shape=[
            pltpu.VMEM(shape, F32) if i in held else jax.ShapeDtypeStruct(shape, F32)
            for i, shape in enumerate(outs)
        ]
        + [pltpu.VMEM(shapes[i], values[i].dtype) for i in keep],
        in_specs=[VMEM if isinstance(x, Held) else ANY for x in arrays],
        out_specs=[VMEM if i in held else ANY for i in range(n_out)] + [VMEM] * len(keep),
        scratch_shapes=[pltpu.VMEM(shapes[i], values[i].dtype) for i in moved]
        + [pltpu.VMEM(outs[i], F32) for i in sent]
        + [pltpu.VMEM(shape, dtype) for shape, dtype in scratch]
        + [
            pltpu.SemaphoreType.DMA((max(len(fetched), 1),)),
            pltpu.SemaphoreType.DMA((max(len(sent), 1),)),
        ],
        compiler_params=pltpu.CompilerParams(vmem_limit_bytes=40 << 20),
        name=name,
    )(*values)
    return [Held(x) if i in held or i >= n_out else x for i, x in enumerate(results)]


def on_device(
    field_prev,
    field_now,
    adjoint_now,
    adjoint_next,
    inv_mass,
    metric,
    connect,
    surface,
    driver,
    shared,
    filter_taps,
    signal,
):
    wide, narrow, narrow_back, weights = (jnp.asarray(t) for t in element_tables())
    count = connect.shape[0]
    peers = shared.shape[2]
    doms = lax.axis_size("dom")
    devices = lax.axis_size(ALL)
    width = filter_taps.shape[1]
    sizes = dict(doms=doms, peers=peers)
    plane = (LANES, LANES)
    now0, now1, prev0, prev1, mass = (
        x.reshape(plane) for x in (field_now, adjoint_now, field_prev, adjoint_next, inv_mass)
    )
    links = shared.reshape(3, peers, NN)
    driver_row = driver.reshape(1, count)
    if width % LANES == 0:
        window, taps, samples = width, filter_taps, signal
    else:
        window = None
        samples = lax.dynamic_slice_in_dim(signal, lax.axis_index(ALL) * width, width, 1)
        pad = ((0, 0), (0, -width % LANES))
        taps, samples = jnp.pad(filter_taps, pad), jnp.pad(samples, pad)

    def trade(x):
        return Held(lax.all_to_all(x.value, ALL, 0, 0, tiled=True))

    def swap(x):
        return Held(lax.ppermute(x.value, "chip", [(0, 1), (1, 0)]))

    nodes = (2,) + plane
    elements = ((2, count, NN), F32)
    sums = ((4 * ROWS, COLS), F32)
    table = ((4 * ROWS, COLS), BF)
    packet = (devices, 1, PACKET)
    terms, connect0, now0_held, now1_held = call(
        drive_kernel,
        "drive",
        [taps, connect, now0, now1, samples],
        [(devices, 8, LANES)],
        [],
        window,
        held=(0,),
        keep=(1, 2, 3),
    )
    drive = trade(terms)
    back, partial, surface0, driver0, links0 = call(
        first_kernel,
        "operator0",
        [connect0, now0_held, now1_held, surface, driver_row, metric, weights, narrow, narrow_back, wide, links],
        [elements[0], (1, LANES)],
        [elements, table],
        held=(0, 1),
        keep=(3, 4, 10),
    )
    local, send = call(
        functools.partial(second_kernel, sizes=sizes),
        "assemble0",
        [drive, surface0, driver0, back, connect0, partial, links0],
        [nodes, packet],
        [elements, sums, table],
        held=(0, 1),
    )
    other = swap(local)
    recv0 = trade(send)
    base, *rest = call(
        base_kernel,
        "base0",
        [local, other, mass, now0, now1, prev0, prev1, links, connect, surface, driver_row]
        + [metric, weights, narrow, narrow_back],
        [nodes],
        [],
        held=(0,),
        keep=(2, 7, 8, 9, 10, 11, 12, 13, 14),
    )
    current, local, send = call(
        functools.partial(third_kernel, sizes=sizes),
        "step1",
        [recv0, base, *rest, wide, drive],
        [nodes, nodes, packet],
        [elements, elements, elements, sums, table],
        held=(0, 1, 2),
    )
    other = swap(local)
    recv1 = trade(send)
    base, mass1, links1, samples1 = call(
        last_base_kernel,
        "base1",
        [local, other, mass, current, now0, now1, links, samples],
        [nodes],
        [],
        window,
        held=(0,),
        keep=(2, 6, 7),
    )
    out0, out1, grad = call(
        functools.partial(last_kernel, sizes=sizes, scale=1.0 / math.sqrt(NN * count * devices)),
        "finish",
        [recv1, base, mass1, links1, recv0, samples1],
        [plane, plane, (8, taps.shape[1])],
        [],
    )
    grad = grad[:, :width]
    return out0.reshape(1, -1), out1.reshape(1, -1), grad


def solution(mesh):
    region = P(("groups", "dom", "sub"), None)
    element = P(("groups", "dom", "sub", "chip"), None)
    in_specs = (
        region,
        region,
        region,
        region,
        region,
        element,
        element,
        element,
        P(("groups", "dom", "sub", "chip")),
        P(("groups", "dom", "sub"), None, None, None),
        P(None, ALL),
        P(),
    )
    out_specs = (region, region, P("groups", ALL))
    return jax.shard_map(
        on_device, mesh=mesh, in_specs=in_specs, out_specs=out_specs, check_vma=False
    )
```

```python
import functools
import math

import jax
import jax.numpy as jnp
import numpy as np
from jax import lax
from jax.experimental import pallas as pl
from jax.experimental.pallas import tpu as pltpu
from jax.sharding import PartitionSpec as P

NN = 512
LANES = 128
ROWS = 64
COLS = 256
BLOCK = 32
PACKET = 2 * NN + LANES
ALL = ("dom", "sub", "chip")

GLL_POINTS = (
    -1.0,
    -0.8717401485096066,
    -0.5917001814331423,
    -0.2092992179024789,
    0.2092992179024789,
    0.5917001814331423,
    0.8717401485096066,
    1.0,
)
GLL_WEIGHTS = (
    0.03571428571428571,
    0.21070422714350603,
    0.3411226924835044,
    0.4124587946587038,
    0.4124587946587038,
    0.3411226924835044,
    0.21070422714350603,
    0.03571428571428571,
)
BF = jnp.bfloat16
F32 = jnp.float32


def element_tables():
    points = np.array(GLL_POINTS)
    identity = np.eye(8)
    diffs = points[:, None] - points[None, :] + identity
    barycentric = 1.0 / np.prod(diffs, axis=1)
    derivative = barycentric[None, :] / barycentric[:, None] / diffs
    derivative = derivative * (1.0 - identity)
    derivative = derivative - identity * derivative.sum(axis=1)[:, None]
    along_x = np.kron(derivative, np.eye(64)).T
    along_y = np.kron(np.eye(4), np.kron(derivative, identity)).T
    along_z = np.kron(np.eye(32), derivative).T
    quad = np.array(GLL_WEIGHTS)
    cube = np.kron(np.kron(quad, quad), quad)

    def parts(table):
        table = table.astype(np.float32)
        high = table.astype(jnp.bfloat16)
        low = (table - high.astype(np.float32)).astype(jnp.bfloat16)
        return high, low

    wide = list(parts(along_x)) + list(parts(along_x.T))
    forward = parts(np.concatenate([along_y, along_z], axis=1))
    backward = parts(np.concatenate([along_y.T, along_z.T], axis=0))
    weights = np.concatenate([cube] * 3).astype(np.float32)[None, :]
    return np.stack(wide), np.stack(forward), np.stack(backward), weights


def halves(x):
    high = x.astype(BF)
    return high, (x - high.astype(F32)).astype(BF)


def mm(a, b):
    return jnp.dot(a, b, preferred_element_type=F32)


def times(x, high, low):
    xh, xl = halves(x)
    rows = x.shape[0]
    both = mm(jnp.concatenate([xh, xl], axis=0), high)
    return both[:rows] + both[rows:] + mm(xh, low)


def stack_halves(x):
    return jnp.concatenate([x[:, :256], x[:, 256:]], axis=0)


def unstack_halves(x):
    rows = x.shape[0] // 2
    return jnp.concatenate([x[:rows], x[rows:]], axis=1)


def split_index(index):
    row = (index >> 7) & (ROWS - 1)
    column = (index & (LANES - 1)) | ((index >> 13) << 7)
    return row, column


def column_hot(column):
    ids = lax.broadcasted_iota(jnp.int32, (COLS, NN), 0).astype(BF)
    return jnp.where(ids == column.astype(BF), BF(1), BF(0))


def fill_table(table_ref, fields):
    for k in range(2):
        field = fields[k]
        plane = jnp.concatenate([field[:ROWS], field[ROWS:]], axis=1)
        high, low = halves(plane)
        table_ref[k * ROWS : (k + 1) * ROWS] = high
        table_ref[(2 + k) * ROWS : (3 + k) * ROWS] = low


def look_up_columns(table, index):
    row, column = split_index(index)
    return mm(table, column_hot(column)), row


def pick_rows(found, row):
    found = found[: 2 * ROWS] + found[2 * ROWS :]
    mask = lax.broadcasted_iota(jnp.int32, (ROWS, NN), 0) == row
    return [
        jnp.sum(jnp.where(mask, found[k * ROWS : (k + 1) * ROWS], 0.0), axis=0, keepdims=True)
        for k in range(2)
    ]


def spread(indices, values):
    columns = []
    placed = []
    ids = lax.broadcasted_iota(jnp.int32, (ROWS, NN), 0).astype(BF)
    for index, pair in zip(indices, values):
        row, column = split_index(index)
        columns.append(column_hot(column))
        mask = ids == row.astype(BF)
        terms = [halves(v) for v in pair]
        placed.append(
            jnp.concatenate(
                [jnp.where(mask, terms[k][s], BF(0)) for s in range(2) for k in range(2)], axis=0
            )
        )
    left = jnp.concatenate(placed, axis=1) if len(placed) > 1 else placed[0]
    right = jnp.concatenate(columns, axis=1) if len(columns) > 1 else columns[0]
    return lax.dot_general(left, right, (((1,), (1,)), ((), ())), preferred_element_type=F32)


def to_fields(sums):
    sums = sums[: 2 * ROWS] + sums[2 * ROWS :]
    return [
        jnp.concatenate(
            [
                sums[k * ROWS : (k + 1) * ROWS, :LANES],
                sums[k * ROWS : (k + 1) * ROWS, LANES:],
            ],
            axis=0,
        )
        for k in range(2)
    ]


def gather_all(table_ref, connect_ref, vals_ref, row):
    count = connect_ref.shape[0]
    table = table_ref[...]
    last = count - 8
    passes = 2
    assert last % passes == 0
    block, rows = last // passes, LANES // passes
    blocks = range(NN // LANES)
    links = [connect_ref[last:, i * LANES : (i + 1) * LANES] for i in blocks]

    def store(e, columns):
        pair = pick_rows(*columns)
        for k in range(2):
            vals_ref[k, pl.ds(e, 1), :] = pair[k]

    def body(i, found):
        found = list(found)
        done = 0
        columns = None
        for u in range(block):
            e = i * block + u
            before = columns
            columns = look_up_columns(table, connect_ref[pl.ds(e, 1), :])
            if before is not None:
                store(e - 1, before)
            upto = rows * (u + 1) // block
            for h in range(done, upto):
                node_row = i * rows + h
                for k in range(2):
                    values = jnp.broadcast_to(row(k, node_row), (8, LANES))
                    for n in blocks:
                        picked = jnp.take_along_axis(
                            values, links[n] & (LANES - 1), axis=1, mode="promise_in_bounds"
                        )
                        at = 2 * n + k
                        found[at] = jnp.where((links[n] >> 7) == node_row, picked, found[at])
            done = upto
        store(i * block + block - 1, columns)
        return tuple(found)

    found = lax.fori_loop(0, passes, body, (jnp.zeros((8, LANES), F32),) * (2 * len(blocks)))
    for n in blocks:
        for k in range(2):
            vals_ref[k, last:, n * LANES : (n + 1) * LANES] = found[2 * n + k]


def operator(vals_ref, metric, weights, narrow, narrow_back, wide, back_ref):
    count = vals_ref.shape[1]
    vals = jnp.concatenate([vals_ref[0], vals_ref[1]], axis=0)
    scale = metric()[...] * weights()[...]
    scale = jnp.concatenate([scale, scale], axis=0)
    along = [scale[:, i * NN : (i + 1) * NN] for i in range(3)]
    split, across, table = narrow(), narrow_back(), wide()
    grads = times(stack_halves(vals), split[0], split[1])
    along_x = times(vals, table[0], table[1])
    grads = grads * jnp.concatenate([stack_halves(x) for x in along[1:]], axis=1)
    along_x = along_x * along[0]
    total = unstack_halves(times(grads, across[0], across[1]))
    total += times(along_x, table[2], table[3])
    back_ref[0] = total[:count]
    back_ref[1] = total[count:]


def driver_hot(driver_ref):
    count = driver_ref.shape[1]
    ids = lax.broadcasted_iota(jnp.int32, (LANES, count), 0)
    return ((ids == driver_ref[...]) & (ids < 8)).astype(F32).T


def driver_sums(vals_ref, surface_ref, hot):
    products = surface_ref[...] * vals_ref[1]
    products = sum(products[:, i * LANES : (i + 1) * LANES] for i in range(NN // LANES))
    return jnp.sum(hot * jnp.sum(products, axis=1, keepdims=True), axis=0, keepdims=True)


def amplitudes(step, drive_ref, hot):
    terms = jnp.sum(drive_ref[...], axis=0)
    half = lax.broadcasted_iota(jnp.int32, (8, LANES), 1) >> 6
    drive = jnp.sum(jnp.where(half == step, terms, 0.0), axis=1, keepdims=True)
    ids = [lax.broadcasted_iota(jnp.int32, (8, LANES), axis) for axis in range(2)]
    row = jnp.sum(jnp.where(ids[0] == ids[1], drive, 0.0), axis=0, keepdims=True)
    return jnp.sum(hot * row, axis=1, keepdims=True)


def residual(amplitude, surface_ref, back_ref, res_ref):
    res_ref[0] = amplitude * surface_ref[...] - back_ref[0]
    res_ref[1] = -back_ref[1]


def scatter_all(res_ref, connect_ref, sums_ref):
    count = connect_ref.shape[0]

    def part(i):
        rows = [pl.ds(i * BLOCK + u, 1) for u in range(BLOCK)]
        return spread(
            [connect_ref[r, :] for r in rows],
            [[res_ref[k, r, :] for k in range(2)] for r in rows],
        )

    if count == BLOCK:
        sums_ref[...] = part(0)
        return
    sums_ref[...] = jnp.zeros_like(sums_ref)

    def body(i, carry):
        sums_ref[...] += part(i)
        return carry

    lax.fori_loop(0, count // BLOCK, body, 0)


def fill_send(table_ref, shared_ref, partial, send_ref, *, doms, peers):
    table = table_ref[...]
    empty = jnp.concatenate([jnp.zeros((1, 2 * NN), F32), partial], axis=1)
    for q in range(send_ref.shape[0]):
        send_ref[q] = empty
    slots = [(o, j) for o in (0, 2, 1) for j in range(peers)]
    columns = [look_up_columns(table, shared_ref[o, j : j + 1, :]) for o, j in slots]
    packets = [jnp.concatenate(pick_rows(*found), axis=1) for found in columns]
    for (o, j), packet in zip(slots, packets):
        dom = jnp.clip(lax.axis_index("dom") + (o - 1), 0, doms - 1)
        for chip in range(2):
            send_ref[(dom * peers + j) * 2 + chip, :, : 2 * NN] = packet


def received_sums(shared_ref, recv_ref, *, doms, peers):
    indices = []
    values = []
    for o in range(3):
        dom = jnp.clip(lax.axis_index("dom") + (o - 1), 0, doms - 1)
        for j in range(peers):
            start = (dom * peers + j) * 2
            both = recv_ref[start] + recv_ref[start + 1]
            indices.append(shared_ref[o, j : j + 1, :])
            values.append([both[:, k * NN : (k + 1) * NN] for k in range(2)])
    total = None
    for at in range(0, len(indices), 8):
        part = spread(indices[at : at + 8], values[at : at + 8])
        total = part if total is None else total + part
    return to_fields(total)


def advance(base, mass, received):
    return [base[k] + mass * received[k] for k in range(2)]


def fill_base(base, current, previous, mass, own, other):
    for k in range(2):
        base[k] = 2.0 * current[k] - previous[k] + mass * (own[k] + other[k])


def base_kernel(ins, outs, scratch):
    own, other, mass, now0, now1, prev0, prev1 = (ref() for ref in ins[:7])
    current, previous = [now0[...], now1[...]], [prev0[...], prev1[...]]
    fill_base(outs[0], current, previous, mass[...], own, other)


def last_base_kernel(ins, outs, scratch):
    own, other, mass, current, now0, now1 = (ref() for ref in ins[:6])
    fill_base(outs[0], current, [now0[...], now1[...]], mass[...], own, other)


def drive_kernel(ins, outs, scratch):
    taps, signal = ins[0](), ins[-1]()
    (send,) = outs
    folded = []
    for t in range(2):
        products = taps[...] * signal[t : t + 1, :]
        products = sum(
            products[:, i * LANES : (i + 1) * LANES] for i in range(products.shape[1] // LANES)
        )
        folded.append(products[:, :64] + products[:, 64:])
    terms = jnp.concatenate(folded, axis=1)
    for q in range(send.shape[0]):
        send[q] = terms


def first_kernel(ins, outs, scratch):
    connect, now0, now1, surface, driver, metric, weights, narrow, narrow_back, wide = ins[:10]
    back, partial = outs
    vals, table = scratch
    fill_table(table, [now0()[...], now1()[...]])
    now = (now0(), now1())
    gather_all(table, connect(), vals, lambda k, r: now[k][pl.ds(r, 1), :])
    operator(vals, metric, weights, narrow, narrow_back, wide, back)
    partial[...] = driver_sums(vals, surface(), driver_hot(driver()))


def local_sums(res, connect, shared, partial, local, send, sums, table, sizes):
    scatter_all(res, connect, sums)
    fields = to_fields(sums[...])
    for k in range(2):
        local[k] = fields[k]
    local.flush()
    fill_table(table, fields)
    fill_send(table, shared, partial, send, **sizes)


def second_kernel(ins, outs, scratch, *, sizes):
    drive, surface, driver, back, connect, partial, shared = ins
    local, send = outs
    res, sums, table = scratch
    residual(amplitudes(0, drive(), driver_hot(driver())), surface(), back(), res)
    local_sums(res, connect(), shared(), partial()[...], local, send, sums, table, sizes)


def third_kernel(ins, outs, scratch, *, sizes):
    recv, base, mass, shared, connect, surface, driver, metric, weights, narrow, narrow_back, wide, drive = ins
    current, local, send = outs
    vals, back, res, sums, table = scratch
    received = received_sums(shared(), recv(), **sizes)
    fields = advance(base(), mass()[...], received)
    for k in range(2):
        current[k] = fields[k]
    current.flush()
    fill_table(table, fields)
    hot = driver_hot(driver())
    amplitude = amplitudes(1, drive(), hot)
    gather_all(table, connect(), vals, lambda k, r: current.buffer[k, pl.ds(r, 1), :])
    operator(vals, metric, weights, narrow, narrow_back, wide, back)
    partial = driver_sums(vals, surface(), hot)
    residual(amplitude, surface(), back, res)
    local_sums(res, connect(), shared(), partial, local, send, sums, table, sizes)


def last_kernel(ins, outs, scratch, *, sizes, scale):
    recv, base, mass, shared, recv_before, signal = ins
    out0, out1, grad = outs
    received = received_sums(shared(), recv(), **sizes)
    fields = advance(base(), mass()[...], received)
    for out, field in zip((out0, out1), fields):
        out[...] = field
        out.flush()

    def column(ref):
        row = sum(ref[q, :, 2 * NN :] for q in range(ref.shape[0]))
        ids = [lax.broadcasted_iota(jnp.int32, (8, LANES), axis) for axis in range(2)]
        row = jnp.where(ids[0] == ids[1], jnp.broadcast_to(row, (8, LANES)), 0.0)
        return jnp.sum(row, axis=1, keepdims=True) * scale

    window = signal()
    grad[...] = column(recv()) * window[0:1, :] + column(recv_before()) * window[1:2, :]


class Input:
    def __init__(self, source, buffer, semaphore):
        self.buffer = buffer
        self.copy = pltpu.make_async_copy(source, buffer, semaphore)
        self.waited = False
        self.copy.start()

    def __call__(self):
        if not self.waited:
            self.copy.wait()
            self.waited = True
        return self.buffer


class Output:
    def __init__(self, target, buffer, semaphore):
        self.buffer = buffer
        self.shape = buffer.shape
        self.copy = None if target is None else pltpu.make_async_copy(buffer, target, semaphore)
        self.sent = False

    def __setitem__(self, index, value):
        self.buffer[index] = value

    def flush(self):
        if self.copy is not None and not self.sent:
            self.copy.start()
            self.sent = True

    def wait(self):
        if self.copy is not None:
            self.copy.wait()


class Held:
    def __init__(self, value):
        self.value = value


ANY = pl.BlockSpec(memory_space=pl.ANY)
VMEM = pl.BlockSpec(memory_space=pltpu.VMEM)


def call(body, name, arrays, outs, scratch, window=None, held=(), keep=()):
    n_in, n_out = len(arrays), len(outs)
    fetched = [i for i, x in enumerate(arrays) if not isinstance(x, Held)]
    moved = [i for i in fetched if i not in keep]
    sent = [i for i in range(n_out) if i not in held]
    values = [
        pltpu.with_memory_space_constraint(x.value, pltpu.VMEM)
        if isinstance(x, Held)
        else pltpu.with_memory_space_constraint(x, pltpu.HBM)
        for x in arrays
    ]
    shapes = [x.shape for x in values]
    if window is not None:
        shapes[-1] = (shapes[-1][0], window)

    def kernel(*refs):
        sources, refs = list(refs[:n_in]), refs[n_in:]
        targets, refs = refs[:n_out], refs[n_out:]
        kept, refs = refs[: len(keep)], refs[len(keep) :]
        in_buffers, refs = refs[: len(moved)], refs[len(moved) :]
        out_buffers, refs = refs[: len(sent)], refs[len(sent) :]
        own, (in_sems, out_sems) = refs[:-2], refs[-2:]
        if window is not None:
            start = pl.multiple_of(lax.axis_index(ALL) * window, LANES)
            sources[-1] = sources[-1].at[:, pl.ds(start, window)]
        ins = [functools.partial(lambda ref: ref, ref) for ref in sources]
        buffers = dict(zip(moved, in_buffers)) | dict(zip(keep, kept))
        for at, i in enumerate(fetched):
            ins[i] = Input(sources[i], buffers[i], in_sems.at[at])
        results = [Output(None, ref, None) for ref in targets]
        for at, i in enumerate(sent):
            results[i] = Output(targets[i], out_buffers[at], out_sems.at[at])
        body(ins, results, own)
        for result in results:
            result.flush()
        for result in results:
            result.wait()
        for value in ins:
            value()

    results = pl.pallas_call(
        kernel,
        out_shape=[
            pltpu.VMEM(shape, F32) if i in held else jax.ShapeDtypeStruct(shape, F32)
            for i, shape in enumerate(outs)
        ]
        + [pltpu.VMEM(shapes[i], values[i].dtype) for i in keep],
        in_specs=[VMEM if isinstance(x, Held) else ANY for x in arrays],
        out_specs=[VMEM if i in held else ANY for i in range(n_out)] + [VMEM] * len(keep),
        scratch_shapes=[pltpu.VMEM(shapes[i], values[i].dtype) for i in moved]
        + [pltpu.VMEM(outs[i], F32) for i in sent]
        + [pltpu.VMEM(shape, dtype) for shape, dtype in scratch]
        + [
            pltpu.SemaphoreType.DMA((max(len(fetched), 1),)),
            pltpu.SemaphoreType.DMA((max(len(sent), 1),)),
        ],
        compiler_params=pltpu.CompilerParams(vmem_limit_bytes=40 << 20),
        name=name,
    )(*values)
    return [Held(x) if i in held or i >= n_out else x for i, x in enumerate(results)]


def on_device(
    field_prev,
    field_now,
    adjoint_now,
    adjoint_next,
    inv_mass,
    metric,
    connect,
    surface,
    driver,
    shared,
    filter_taps,
    signal,
):
    wide, narrow, narrow_back, weights = (jnp.asarray(t) for t in element_tables())
    count = connect.shape[0]
    peers = shared.shape[2]
    doms = lax.axis_size("dom")
    devices = lax.axis_size(ALL)
    width = filter_taps.shape[1]
    sizes = dict(doms=doms, peers=peers)
    plane = (LANES, LANES)
    now0, now1, prev0, prev1, mass = (
        x.reshape(plane) for x in (field_now, adjoint_now, field_prev, adjoint_next, inv_mass)
    )
    links = shared.reshape(3, peers, NN)
    driver_row = driver.reshape(1, count)
    if width % LANES == 0:
        window, taps, samples = width, filter_taps, signal
    else:
        window = None
        samples = lax.dynamic_slice_in_dim(signal, lax.axis_index(ALL) * width, width, 1)
        pad = ((0, 0), (0, -width % LANES))
        taps, samples = jnp.pad(filter_taps, pad), jnp.pad(samples, pad)

    def trade(x):
        return Held(lax.all_to_all(x.value, ALL, 0, 0, tiled=True))

    def swap(x):
        return Held(lax.ppermute(x.value, "chip", [(0, 1), (1, 0)]))

    nodes = (2,) + plane
    elements = ((2, count, NN), F32)
    sums = ((4 * ROWS, COLS), F32)
    table = ((4 * ROWS, COLS), BF)
    packet = (devices, 1, PACKET)
    terms, connect0, now0_held, now1_held = call(
        drive_kernel,
        "drive",
        [taps, connect, now0, now1, samples],
        [(devices, 8, LANES)],
        [],
        window,
        held=(0,),
        keep=(1, 2, 3),
    )
    drive = trade(terms)
    back, partial, surface0, driver0, links0 = call(
        first_kernel,
        "operator0",
        [connect0, now0_held, now1_held, surface, driver_row, metric, weights, narrow, narrow_back, wide, links],
        [elements[0], (1, LANES)],
        [elements, table],
        held=(0, 1),
        keep=(3, 4, 10),
    )
    local, send = call(
        functools.partial(second_kernel, sizes=sizes),
        "assemble0",
        [drive, surface0, driver0, back, connect0, partial, links0],
        [nodes, packet],
        [elements, sums, table],
        held=(0, 1),
    )
    other = swap(local)
    recv0 = trade(send)
    base, *rest = call(
        base_kernel,
        "base0",
        [local, other, mass, now0, now1, prev0, prev1, links, connect, surface, driver_row]
        + [metric, weights, narrow, narrow_back],
        [nodes],
        [],
        held=(0,),
        keep=(2, 7, 8, 9, 10, 11, 12, 13, 14),
    )
    current, local, send = call(
        functools.partial(third_kernel, sizes=sizes),
        "step1",
        [recv0, base, *rest, wide, drive],
        [nodes, nodes, packet],
        [elements, elements, elements, sums, table],
        held=(0, 1, 2),
    )
    other = swap(local)
    recv1 = trade(send)
    base, mass1, links1, samples1 = call(
        last_base_kernel,
        "base1",
        [local, other, mass, current, now0, now1, links, samples],
        [nodes],
        [],
        window,
        held=(0,),
        keep=(2, 6, 7),
    )
    out0, out1, grad = call(
        functools.partial(last_kernel, sizes=sizes, scale=1.0 / math.sqrt(NN * count * devices)),
        "finish",
        [recv1, base, mass1, links1, recv0, samples1],
        [plane, plane, (8, taps.shape[1])],
        [],
    )
    grad = grad[:, :width]
    return out0.reshape(1, -1), out1.reshape(1, -1), grad


def solution(mesh):
    region = P(("groups", "dom", "sub"), None)
    element = P(("groups", "dom", "sub", "chip"), None)
    in_specs = (
        region,
        region,
        region,
        region,
        region,
        element,
        element,
        element,
        P(("groups", "dom", "sub", "chip")),
        P(("groups", "dom", "sub"), None, None, None),
        P(None, ALL),
        P(),
    )
    out_specs = (region, region, P("groups", ALL))
    return jax.shard_map(
        on_device, mesh=mesh, in_specs=in_specs, out_specs=out_specs, check_vma=False
    )
```
